32 devices in a mesh: groups: 2 (over y), ctx: 4 (over z), pair: 2 (over x), tp: 2 (over core).
Axes of the slice: x: 2, y: 2, z: 4, core: 2. Of those that a mesh axis runs over, the one named last changes fastest.
Arguments:
- queries: bfloat16 [4096, 16, 128], P(('groups', 'ctx'), ('pair', 'tp')), parts along dimension 0, may hold values from -5 to 5
- keys: bfloat16 [4096, 4, 128], P(('groups', 'ctx', 'tp'), 'pair'), parts along dimension 0, may hold values from -5 to 5
- values: bfloat16 [4096, 4, 128], P(('groups', 'ctx', 'tp'), 'pair'), parts along dimension 0, may hold values from -6 to 6
- span_order: int32 [8], P('groups'), parts along dimension 0, may hold values from 0 to 3, each once
- lengths: int32 [8], P('groups'), parts along dimension 0, may hold values from 1 to 1024, 2048 in all
- kv_partner: int32 [32, 1], P('groups'), parts along dimension 0, may hold values from 0 to 3; in each aligned block of 16 rows (0 to 15, 16 to 31, ...) at most 8 rows name the same one
Outputs:
- attended: bfloat16 [4096, 16, 128], P(('groups', 'ctx'), ('pair', 'tp')), parts along dimension 0
- decode_cache: bfloat16 [64, 2, 128, 4, 128], P(('groups', 'ctx'), None, ('pair', 'tp')), parts along dimension 0
The draws below stay inside these ranges and needn't reach their ends.
There are 2 independent parts, one for each index of `groups`. The reference program is written for one: setup_inputs(seed, part) draws one part's arguments, and reference() takes and returns one part's arrays. A program takes and returns all parts, laid end to end along the dimension named above; each array names one. Nothing has to cross between parts.
Inputs may be any that keep to these rules, and one draw needn't show every extreme that they name: The lengths sum to 2048; the largest is exactly 1024. `kv_partner`: no decode partner is named by more than 8 blocks, a bound that some block reaches.
All inputs are finite; a program needn't handle non-finite values.
Results may differ from the reference program's by a relative error of at most 0.0037.
Values may be sent and summed in bfloat16 or wider, within the bound.
No kernel may reach another device: no remote copies, remote signals or barrier semaphores. Data moves between devices by JAX's collectives and lax.ppermute only.
A program may use at most 64 MiB of HBM per device.

```python
import math
import jax
import jax.numpy as jnp
import numpy as np
from jax import lax

HQ = 16
KVH = 4
HD = 128
GROUP = 4
HALF = 256
BLK = 128
NREQ = 4
SHARDS = 4
SPANS = 8
SEQ = 2048
NBLK = 16
CAP = 8


def draw_queries(key, part):
    key = jax.random.fold_in(key, 11)
    return jnp.clip(jax.random.normal(key, (SEQ, HQ, HD), jnp.float32), -5.0, 5.0).astype(jnp.bfloat16)


def draw_keys(key, part):
    key = jax.random.fold_in(key, 23)
    return jnp.clip(jax.random.normal(key, (SEQ, KVH, HD), jnp.float32), -5.0, 5.0).astype(jnp.bfloat16)


def steps_of(key, dims, pieces, low, high):
    factor_of, own = 1.0, jax.random.fold_in(key, 6)
    for axis_at, shards_of in pieces:
        draws = jnp.exp(jax.random.uniform(jax.random.fold_in(own, axis_at), (shards_of,), jnp.float32, low / len(pieces), high / len(pieces)))
        factor_of = factor_of * jnp.repeat(draws, dims[axis_at] // shards_of).reshape([-1 if axis == axis_at else 1 for axis in range(len(dims))])
    return factor_of


def length_profile(amount, total, limit, lean):
    loads = [(1 << 20) // math.isqrt(grade ** lean) + 1 for grade in range(2, amount + 1)]
    rest, counts = total - limit - (amount - 1), [1] * (amount - 1)
    while rest > 0:
        candidates = [i for i in range(amount - 1) if counts[i] < limit]
        mass, remaining = sum([loads[i] for i in candidates]), rest
        for i in candidates:
            extra = min(limit - counts[i], max(1, remaining * loads[i] // mass), rest)
            counts[i] = counts[i] + extra
            rest = rest - extra
    return np.array([limit] + counts)


def uneven(own_key, count, total, most, skew):
    if count == 2:
        one = jax.random.randint(own_key, (), max(1, total - most), min(most, total - 1) + 1)
        return jnp.stack([one, total - one])
    sizes = jnp.asarray(length_profile(count, total, most, skew), jnp.int32)
    couples = (count - 1) // 2
    donor, sink = sizes[1:1 + 2 * couples:2], sizes[2:2 + 2 * couples:2]
    slack = jnp.minimum(donor - 1, most - sink)
    moved = jax.random.randint(jax.random.fold_in(own_key, 1), (couples,), 0, 1 << 20) % (slack + 1)
    sizes = sizes.at[1:1 + 2 * couples:2].set(donor - moved).at[2:2 + 2 * couples:2].set(sink + moved)
    return sizes[jax.random.permutation(jax.random.fold_in(own_key, 2), count)]


def assign_block(own_key, own, number, rows, number_of, top, bound, lean):
    order = jax.random.permutation(own_key, number_of)
    packed, common = portions_of(number_of, rows * top, bound, lean, True), portions_of(number_of, rows * top, bound, lean, False)
    places = jnp.arange(number_of)

    def named(tallies, turn):
        used = int((tallies > 0).sum())
        fixed = max(1, used // 4)
        passed = fixed + (places - fixed + turn * (used - fixed)) % max(1, number_of - fixed)
        return jnp.zeros((number_of,), jnp.int32).at[order[jnp.where(places < fixed, places, passed)]].set(jnp.asarray(tallies, jnp.int32))

    tallies = jnp.where(number % 4 == 0, named(packed, number // 4), named(common, number - number // 4 - 1))
    mixed = jax.random.permutation(jax.random.fold_in(own, 3), number_of)
    giver, taker = mixed[0:number_of // 2 * 2:2], mixed[1:number_of // 2 * 2:2]
    room = jnp.minimum(tallies[giver] - 1, bound - tallies[taker]) // 2
    room = jnp.where((giver == order[0]) | (taker == order[0]) | (tallies[taker] == 0), 0, jnp.maximum(room, 0))
    passed = jax.random.randint(jax.random.fold_in(own, 4), (number_of // 2,), 0, 1 << 20) % (room + 1)
    tallies = tallies.at[giver].add(-passed).at[taker].add(passed)
    labels = jnp.searchsorted(jnp.cumsum(tallies), jnp.arange(rows * top), side="right").astype(jnp.int32)
    listing = labels.reshape(top, rows).T
    listing = listing[jax.random.permutation(jax.random.fold_in(own, 1), rows)]
    turn = jax.random.randint(jax.random.fold_in(own, 2), (rows, 1), 0, top)
    return jnp.take_along_axis(listing, (jnp.arange(top)[None, :] + turn) % top, axis=1)


def portions_of(number_of, total, reach, lean, full):
    portions = [(1 << 20) // math.isqrt(standing ** lean) + 1 for standing in range(1, number_of + 1)]
    largest = reach if full else min(reach, max(-(-total // number_of), total * portions[0] // sum(portions)))
    least = 1 if total - largest >= number_of - 1 else 0
    holding, surplus = [largest] + [least] * (number_of - 1), total - largest - least * (number_of - 1)
    while surplus > 0:
        free = [i for i in range(1, number_of) if holding[i] < largest] or [i for i in range(1, number_of) if holding[i] < reach]
        pool, left = sum([portions[i] for i in free]), surplus
        for i in free:
            more = min(reach - holding[i], max(1, left * portions[i] // pool), surplus)
            holding[i] = holding[i] + more
            surplus = surplus - more
    return np.array(holding)


def gaussian(rng, shape, deviation, reach, split=(), kind=jnp.bfloat16):
    array = deviation * jax.random.normal(rng, shape, jnp.float32)
    if split:
        array = array * steps_of(rng, shape, split, -0.22, 0.18)
    return jnp.clip(array, -reach, reach).astype(kind)


def setup_inputs(seed: int = 0, part: int = 0) -> dict:
    seeds = jax.random.split(jax.random.key(seed), 7)
    part_keys = jax.random.split(jax.random.fold_in(seeds[6], part), 7)
    queries = draw_queries(jax.random.fold_in(jax.random.fold_in(seeds[6], part), 71), part)
    keys = draw_keys(jax.random.fold_in(jax.random.fold_in(seeds[6], part), 71), part)
    values = gaussian(part_keys[2], (SEQ, KVH, HD), 1.0, 6.0, ((0, 8), (1, 2)))
    span_order = jax.random.permutation(part_keys[3], SHARDS).astype(jnp.int32)
    lengths = uneven(part_keys[4], NREQ, SEQ, SEQ // 2, 2).astype(jnp.int32)
    kv_partner_keys = jax.random.split(jax.random.fold_in(part_keys[5], 1), NBLK // NBLK)
    kv_partner_turns = jax.random.permutation(jax.random.fold_in(part_keys[5], 3), NBLK // NBLK)
    kv_partner = jax.vmap(lambda own, number: assign_block(jax.random.fold_in(part_keys[5], 2), own, number, NBLK, SHARDS, 1, CAP, 2))(kv_partner_keys, kv_partner_turns).reshape((NBLK, 1))
    return {"queries": queries, "keys": keys, "values": values, "span_order": span_order, "lengths": lengths, "kv_partner": kv_partner}


def buffer_positions(span_order):
    row_index = jnp.arange(SEQ, dtype=jnp.int32)
    block_index = row_index // HALF
    leading = span_order[block_index // 2]
    span_index = jnp.where(block_index % 2 == 0, leading, SPANS - 1 - leading)
    return (span_index * HALF + row_index % HALF).astype(jnp.int32)


def request_index(position, lengths):
    boundary = jnp.cumsum(lengths).astype(jnp.int32)
    return jnp.sum((boundary[None, :] <= position[:, None]).astype(jnp.int32), axis=1)


def reference(queries, keys, values, span_order, lengths, kv_partner):
    position = buffer_positions(span_order)
    row_index = jnp.arange(SEQ, dtype=jnp.int32)
    row_of = jnp.zeros((SEQ,), jnp.int32).at[position].set(row_index)
    ordered_q = queries[row_of]
    ordered_k = keys[row_of]
    ordered_v = values[row_of]
    request = request_index(row_index, lengths)
    scale = HD ** -0.5
    block_rows = 2 * HALF
    block_count = SEQ // block_rows

    def key_block(number):
        begin = number * block_rows
        key_part = lax.dynamic_slice_in_dim(ordered_k, begin, block_rows, 0).astype(jnp.float32)
        value_part = lax.dynamic_slice_in_dim(ordered_v, begin, block_rows, 0).astype(jnp.float32)
        return jnp.repeat(key_part, GROUP, axis=1), jnp.repeat(value_part, GROUP, axis=1)

    def visible_mask(query_begin, key_begin):
        query_pos = query_begin + jnp.arange(block_rows, dtype=jnp.int32)
        key_pos = key_begin + jnp.arange(block_rows, dtype=jnp.int32)
        query_req = lax.dynamic_slice_in_dim(request, query_begin, block_rows, 0)
        key_req = lax.dynamic_slice_in_dim(request, key_begin, block_rows, 0)
        return (key_pos[None, :] <= query_pos[:, None]) & (key_req[None, :] == query_req[:, None])

    def query_block(number):
        query_begin = number * block_rows
        query_part = lax.dynamic_slice_in_dim(ordered_q, query_begin, block_rows, 0).astype(jnp.float32)

        def peak_step(key_number, peak):
            visible = visible_mask(query_begin, key_number * block_rows)

            def update(current):
                key_exp, _ = key_block(key_number)
                scores = jnp.einsum("rhd,nhd->rhn", query_part, key_exp) * scale
                scores = jnp.where(visible[:, None, :], scores, -jnp.inf)
                return jnp.maximum(current, jnp.max(scores, axis=2))

            return lax.cond(jnp.any(visible), update, lambda current: current, peak)

        peak = lax.fori_loop(0, block_count, peak_step, jnp.full((block_rows, HQ), -jnp.inf, jnp.float32))

        def sum_step(key_number, carry):
            total, summed = carry
            visible = visible_mask(query_begin, key_number * block_rows)

            def update(current):
                total_now, summed_now = current
                key_exp, value_exp = key_block(key_number)
                scores = jnp.einsum("rhd,nhd->rhn", query_part, key_exp) * scale
                weights = jnp.where(visible[:, None, :], jnp.exp(jnp.where(visible[:, None, :], scores, -jnp.inf) - peak[:, :, None]), 0.0)
                rounded = lax.optimization_barrier(weights.astype(jnp.bfloat16)).astype(jnp.float32)
                return (total_now + jnp.sum(weights, axis=2), summed_now + jnp.einsum("rhn,nhd->rhd", rounded, value_exp))

            return lax.cond(jnp.any(visible), update, lambda current: current, (total, summed))

        start_carry = (jnp.zeros((block_rows, HQ), jnp.float32), jnp.zeros((block_rows, HQ, HD), jnp.float32))
        total, summed = lax.fori_loop(0, block_count, sum_step, start_carry)
        return (summed / total[:, :, None]).astype(jnp.bfloat16)

    attended_ordered = lax.map(query_block, jnp.arange(block_count, dtype=jnp.int32)).reshape(SEQ, HQ, HD)
    attended = attended_ordered[position]

    partner = kv_partner[:, 0]
    block_index = jnp.arange(NBLK, dtype=jnp.int32)
    same = (partner[None, :] == partner[:, None]) & (block_index[None, :] < block_index[:, None])
    rank = jnp.sum(same.astype(jnp.int32), axis=1)
    slot = (partner * CAP + rank).astype(jnp.int32)
    blocks = jnp.stack([ordered_k, ordered_v], axis=1).reshape(NBLK, BLK, 2, KVH, HD).transpose(0, 2, 1, 3, 4)
    decode_cache = jnp.zeros((SHARDS * CAP, 2, BLK, KVH, HD), jnp.bfloat16).at[slot].set(blocks)
    return attended, decode_cache
```

```python
import functools

import jax
import jax.numpy as jnp
from jax import lax
from jax.experimental import pallas as pl
from jax.experimental.pallas import tpu as pltpu
from jax.sharding import PartitionSpec as P

GROUP = 4
BLK = 128
CAP = 8


neg_big = -1e30
key_block = 1024


def lookup(entries, where_at):
    entry_count = entries.shape[0]
    matches = where_at[..., None] == jnp.arange(entry_count, dtype=jnp.int32)
    return jnp.sum(jnp.where(matches, entries, 0), axis=-1)


def row_position(row_index, span_order, span_total, half_rows):
    block_index = row_index // half_rows
    leading = lookup(span_order, block_index // 2)
    span_index = jnp.where(block_index % 2 == 0, leading, span_total - 1 - leading)
    return span_index * half_rows + row_index % half_rows


def position_row(position, span_order, span_total, half_rows):
    span_index = position // half_rows
    shard_index = jnp.arange(span_order.shape[0], dtype=jnp.int32)
    even_match = span_order == span_index[..., None]
    odd_match = span_total - 1 - span_order == span_index[..., None]
    block_index = jnp.sum(
        jnp.where(even_match, 2 * shard_index, 0) + jnp.where(odd_match, 2 * shard_index + 1, 0),
        axis=-1,
    )
    return block_index * half_rows + position % half_rows


def request_of(position, lengths):
    boundary = jnp.cumsum(lengths)
    return jnp.sum((boundary <= position[..., None]).astype(jnp.int32), axis=-1)


def keep_state(inner):
    return inner


def shards(queries, keys, values, span_order, lengths, kv_partner):
    pair_count = lax.axis_size("pair")
    core_count = lax.axis_size("tp")
    span_total = 2 * lax.axis_size("ctx")
    ctx_index = lax.axis_index("ctx")
    core_index = lax.axis_index("tp")
    query_rows, local_heads, head_width = queries.shape
    half_rows = query_rows // 2
    local_groups = keys.shape[1]
    scale = head_width ** (-0.5)
    query_pos = row_position(
        ctx_index * query_rows + jnp.arange(query_rows, dtype=jnp.int32),
        span_order,
        span_total,
        half_rows,
    )
    query_req = request_of(query_pos, lengths)
    partner = kv_partner[:, 0]
    block_index = jnp.arange(partner.shape[0], dtype=jnp.int32)
    earlier = (partner[None, :] == partner[:, None]) & (block_index[None, :] < block_index[:, None])
    rank = jnp.sum(earlier.astype(jnp.int32), axis=1)
    slot_index = jnp.arange(CAP, dtype=jnp.int32)
    taken = (partner[None, :] == ctx_index) & (rank[None, :] == slot_index[:, None])
    slot_live = jnp.any(taken, axis=1)
    slot_block = jnp.sum(jnp.where(taken, block_index[None, :], 0), axis=1)
    token_share = BLK // (pair_count * core_count)
    pair_index = jnp.arange(pair_count, dtype=jnp.int32)

    def make_absorb(query_block, kv_pick, gathered_row, target, live):

        def attend(state, block_keys, block_values, key_rows):
            key_pos = row_position(key_rows, span_order, span_total, half_rows)
            key_req = request_of(key_pos, lengths)
            visible = (key_pos[None, :] <= query_pos[:, None]) & (
                key_req[None, :] == query_req[:, None]
            )

            def update(inner):
                peak, total, summed = inner
                head_keys = jnp.take(block_keys, kv_pick, axis=1)
                head_values = jnp.take(block_values, kv_pick, axis=1)
                scores = (
                    jnp.einsum(
                        "rhd,nhd->rhn", query_block, head_keys, preferred_element_type=jnp.float32
                    )
                    * scale
                )
                scores = jnp.where(visible[:, None, :], scores, neg_big)
                new_peak = jnp.maximum(peak, jnp.max(scores, axis=2))
                weights = jnp.where(
                    visible[:, None, :], jnp.exp(scores - new_peak[:, :, None]), 0.0
                )
                factor = jnp.exp(peak - new_peak)
                new_total = total * factor + jnp.sum(weights, axis=2)
                product = jnp.einsum(
                    "rhn,nhd->rhd",
                    weights.astype(jnp.bfloat16),
                    head_values,
                    preferred_element_type=jnp.float32,
                )
                return (new_peak, new_total, summed * factor[:, :, None] + product)

            return lax.cond(jnp.any(visible), update, keep_state, state)

        def absorb(carry, piece, start):
            state, selected = carry
            piece_keys, piece_values = piece
            count = piece_keys.shape[0]
            inside = live & (target >= 0) & (target < count)
            safe = jnp.clip(target, 0, count - 1)
            picked = jnp.stack(
                [jnp.take(piece_keys, safe, axis=0), jnp.take(piece_values, safe, axis=0)], axis=1
            )
            selected = jnp.where(
                inside[:, None, :, :, :, None, None], picked, jnp.zeros((), jnp.bfloat16)
            )
            turns = count // key_block
            shaped_keys = piece_keys.reshape(turns, key_block, local_groups, head_width)
            shaped_values = piece_values.reshape(turns, key_block, local_groups, head_width)
            block_starts = key_block * jnp.arange(turns, dtype=jnp.int32)

            def one_block(inner, items):
                block_keys, block_values, block_start = items
                key_rows = gathered_row(block_start + jnp.arange(key_block, dtype=jnp.int32))
                return (attend(inner, block_keys, block_values, key_rows), None)

            state, _ = lax.scan(one_block, state, (shaped_keys, shaped_values, block_starts))
            return (state, selected)

        return absorb

    def same_rows(row_index):
        return row_index

    kv_pick = (core_index * local_heads + jnp.arange(local_heads, dtype=jnp.int32)) // GROUP
    ranges = pair_index[:, None] * core_count + jnp.reshape(core_index, (1,))[None, :]
    wanted = (
        slot_block[:, None, None, None] * BLK
        + ranges[None, :, :, None] * token_share
        + jnp.arange(token_share, dtype=jnp.int32)[None, None, None, :]
    )
    target = position_row(wanted, span_order, span_total, half_rows)
    live = jnp.broadcast_to(slot_live[:, None, None, None], target.shape)
    absorb = make_absorb(queries, kv_pick, same_rows, target, live)
    state = (
        jnp.full((query_rows, local_heads), neg_big, jnp.float32),
        jnp.zeros((query_rows, local_heads), jnp.float32),
        jnp.zeros((query_rows, local_heads, head_width), jnp.float32),
    )
    selected = jnp.zeros(
        target.shape[:1] + (2,) + target.shape[1:] + (local_groups, head_width), jnp.bfloat16
    )
    (peak, total, summed), selected = absorb(
        (state, selected),
        (
            lax.all_gather(keys, ("ctx", "tp"), axis=0, tiled=True),
            lax.all_gather(values, ("ctx", "tp"), axis=0, tiled=True),
        ),
        jnp.int32(0),
    )
    selected = selected[:, :, :, 0]
    attended = (summed / total[:, :, None]).astype(jnp.bfloat16)
    received = lax.all_to_all(selected, "pair", split_axis=2, concat_axis=4, tiled=True)
    decode_cache = received.reshape(CAP, 2, token_share, pair_count * local_groups, head_width)
    return (attended, decode_cache)


HALF_TOKENS = BLK // 2
LOG2E = 1.4426950408889634
MASKED = -1e30
FLOOR = -1e29
Q_TILE = 512


def span_of(order_ref, shard, half, span_total):
    leading = order_ref[shard]
    return leading if half == 0 else span_total - 1 - leading


def split_kernel(key_a, key_b, value_a, value_b, cross_ref, stay_ref, wide):
    pair = lax.axis_index("pair")
    core = lax.axis_index("tp")
    for kind, (own, other) in enumerate(((key_a, key_b), (value_a, value_b))):
        wide[kind, core] = own[...].astype(jnp.float32)
        wide[kind, 1 - core] = other[...].astype(jnp.float32)
    for kind in range(2):
        for block in range(4):
            for out, part in ((cross_ref, 1 - pair), (stay_ref, pair)):
                first = (block % 2) * 2 * BLK + part * 2 * HALF_TOKENS + core
                rows = wide[kind, block // 2, pl.ds(first, HALF_TOKENS, stride=2), :]
                out[kind, pl.ds(block * HALF_TOKENS, HALF_TOKENS), :] = rows.astype(jnp.bfloat16)


def split_heads(keys, keys_other, values, values_other):
    rows = keys.shape[0]
    piece = jax.ShapeDtypeStruct((2, rows // 2, keys.shape[1]), jnp.bfloat16)
    return pl.pallas_call(
        split_kernel,
        out_shape=(piece, piece),
        scratch_shapes=[pltpu.VMEM((2, 2, rows, keys.shape[1]), jnp.float32)],
        name="split_heads",
    )(keys, keys_other, values, values_other)


def attend_kernel(sources, first, last, shard_count, heads, *refs):
    order_ref, lengths_ref, query_ref = refs[:3]
    refs = refs[3:]
    pieces, refs = refs[: len(sources)], refs[len(sources) :]
    if not first:
        peak_in, total_in, summed_in = refs[:3]
        refs = refs[3:]
    if last:
        out_ref, peak_ref, total_ref, summed_ref = refs
    else:
        peak_ref, total_ref, summed_ref = refs
    shard = lax.axis_index("ctx")
    pair = lax.axis_index("pair")
    span_total = 2 * shard_count
    rows, width = query_ref.shape
    tokens = rows // heads
    half_rows = tokens // 2
    factor = LOG2E * width**-0.5
    starts = [jnp.int32(0)]
    for r in range(lengths_ref.shape[0] - 1):
        starts.append(starts[-1] + lengths_ref[r])

    def begin_of(position):
        begin = jnp.zeros_like(position)
        for start in starts[1:]:
            begin = jnp.where(start <= position, start, begin)
        return begin

    if first:
        peak_ref[...] = jnp.full(peak_ref.shape, FLOOR, jnp.float32)
        total_ref[...] = jnp.zeros(total_ref.shape, jnp.float32)
        summed_ref[...] = jnp.zeros(summed_ref.shape, jnp.float32)
    else:
        peak_ref[...] = peak_in[...]
        total_ref[...] = total_in[...]
        summed_ref[...] = summed_in[...]

    tile_tokens = Q_TILE // heads
    tiles_half = half_rows // tile_tokens

    def tile(index, _):
        at = pl.multiple_of(index * Q_TILE, Q_TILE)
        columns = pl.ds(at, Q_TILE)
        own_lead = order_ref[shard]
        query_span = jnp.where(index < tiles_half, own_lead, span_total - 1 - own_lead)
        first_pos = query_span * half_rows + lax.rem(index, tiles_half) * tile_tokens
        offset = lax.broadcasted_iota(jnp.int32, (1, Q_TILE), 1) // heads
        query_pos = first_pos + offset
        query_begin = begin_of(query_pos)
        begin_low = begin_of(first_pos)
        for (shift, cross), piece in zip(sources, pieces):
            source = lax.rem(shard + shift, shard_count)
            lead = order_ref[source]
            part = (1 - pair) if cross else pair
            piece_half = piece.shape[1] // 2
            for half in range(2):
                key_span = lead if half == 0 else span_total - 1 - lead
                key_first = key_span * half_rows
                near = (key_first <= first_pos + tile_tokens - 1) & (
                    key_first + half_rows - 1 >= begin_low
                )

                @pl.when(near)
                def _():
                    key_rows = piece[0, pl.ds(half * piece_half, piece_half), :]
                    value_rows = piece[1, pl.ds(half * piece_half, piece_half), :]
                    scores = lax.dot_general(
                        key_rows,
                        query_ref[columns, :],
                        (((1,), (1,)), ((), ())),
                        preferred_element_type=jnp.float32,
                    )
                    local = lax.broadcasted_iota(jnp.int32, (piece_half, 1), 0)
                    key_pos = (
                        key_first
                        + part * HALF_TOKENS
                        + local
                        + jnp.where(local >= HALF_TOKENS, BLK - HALF_TOKENS, 0)
                    )
                    visible = (key_pos <= query_pos) & (key_pos >= query_begin)
                    scores = jnp.where(visible, scores, MASKED)
                    old_peak = peak_ref[:, columns]
                    peak = jnp.maximum(old_peak, jnp.max(scores, axis=0, keepdims=True))
                    weights = jnp.exp2((scores - peak) * factor)
                    fade = jnp.exp2((old_peak - peak) * factor)
                    peak_ref[:, columns] = peak
                    total_ref[:, columns] = total_ref[:, columns] * fade + jnp.sum(
                        weights, axis=0, keepdims=True
                    )
                    product = lax.dot_general(
                        value_rows,
                        weights.astype(jnp.bfloat16),
                        (((0,), (0,)), ((), ())),
                        preferred_element_type=jnp.float32,
                    )
                    summed_ref[:, columns] = summed_ref[:, columns] * fade + product

        if last:
            result = summed_ref[:, columns] / total_ref[:, columns]
            out_ref[columns, :] = jnp.transpose(result).astype(jnp.bfloat16)
        return 0

    lax.fori_loop(0, rows // Q_TILE, tile, 0)


def attend(order, lengths, query, pieces, sources, state, last, shard_count, heads):
    rows, width = query.shape
    first = state is None
    smem = pl.BlockSpec(memory_space=pltpu.SMEM)
    vmem = pl.BlockSpec(memory_space=pltpu.VMEM)
    shapes = [((1, rows), jnp.float32), ((1, rows), jnp.float32), ((width, rows), jnp.float32)]
    state = () if first else state
    if last:
        out_shape = jax.ShapeDtypeStruct((rows, width), jnp.bfloat16)
        scratch = [pltpu.VMEM(s, d) for s, d in shapes]
        out_specs = vmem
    else:
        out_shape = tuple(jax.ShapeDtypeStruct(s, d) for s, d in shapes)
        scratch = []
        out_specs = (vmem,) * 3
    keys_seen = sum(p.shape[1] for p in pieces)
    return pl.pallas_call(
        functools.partial(attend_kernel, sources, first, last, shard_count, heads),
        out_shape=out_shape,
        in_specs=[smem, smem] + [vmem] * (1 + len(pieces) + len(state)),
        out_specs=out_specs,
        scratch_shapes=scratch,
        cost_estimate=pl.CostEstimate(
            flops=2 * rows * width * keys_seen,
            bytes_accessed=4 * rows * width,
            transcendentals=rows * keys_seen // 2,
        ),
        name="attend",
    )(order, lengths, query, *pieces, *state)


def find_slots(order_ref, partner_ref, block_at, shard, shard_count):
    for slot in range(CAP):
        block_at[slot] = -1
    taken = jnp.int32(0)
    for block in range(partner_ref.shape[0]):
        mine = partner_ref[block] == shard

        @pl.when(mine)
        def _():
            block_at[taken] = block

        taken = taken + mine.astype(jnp.int32)


def locate(order_ref, block, shard, shard_count):
    span = block // 2
    source = jnp.int32(0)
    half = jnp.int32(0)
    for index in range(shard_count):
        lead = order_ref[index]
        source = jnp.where((lead == span) | (2 * shard_count - 1 - lead == span), index, source)
        half = jnp.where(2 * shard_count - 1 - lead == span, 1, half)
    return lax.rem(source - shard + shard_count, shard_count), half * 2 + lax.rem(block, 2)


def pick_kernel(shard_count, order_ref, partner_ref, *refs):
    stay, cross = refs[:shard_count], refs[shard_count : 2 * shard_count]
    out_ref, block_at = refs[2 * shard_count :]
    shard = lax.axis_index("ctx")
    core = lax.axis_index("tp")
    share = HALF_TOKENS // 2
    find_slots(order_ref, partner_ref, block_at, shard, shard_count)
    for slot in range(CAP):
        block = block_at[slot]
        shift, place = locate(order_ref, jnp.maximum(block, 0), shard, shard_count)
        begin = pl.multiple_of(place * HALF_TOKENS + (1 - core) * share, share)

        for index in range(shard_count):

            @pl.when((block >= 0) & (shift == index))
            def _():
                for which, group in enumerate((stay, cross)):
                    for kind in range(2):
                        out_ref[slot, kind, which] = group[index][kind, pl.ds(begin, share), :]

        @pl.when(block < 0)
        def _():
            out_ref[slot] = jnp.zeros(out_ref.shape[1:], out_ref.dtype)


def pick(order, partner, stay, cross, shard_count):
    smem = pl.BlockSpec(memory_space=pltpu.SMEM)
    vmem = pl.BlockSpec(memory_space=pltpu.VMEM)
    share = HALF_TOKENS // 2
    return pl.pallas_call(
        functools.partial(pick_kernel, shard_count),
        out_shape=jax.ShapeDtypeStruct((CAP, 2, 2, share, stay[0].shape[2]), jnp.bfloat16),
        in_specs=[smem, smem] + [vmem] * (2 * shard_count),
        out_specs=vmem,
        scratch_shapes=[pltpu.SMEM((CAP,), jnp.int32)],
        name="pick_slots",
    )(order, partner, *stay, *cross)


def place_kernel(shard_count, order_ref, partner_ref, *refs):
    stay, cross = refs[:shard_count], refs[shard_count : 2 * shard_count]
    given_ref, out_ref, block_at, wide = refs[2 * shard_count :]
    shard = lax.axis_index("ctx")
    pair = lax.axis_index("pair")
    core = lax.axis_index("tp")
    share = HALF_TOKENS // 2
    find_slots(order_ref, partner_ref, block_at, shard, shard_count)
    for slot in range(CAP):
        block = block_at[slot]
        shift, place = locate(order_ref, jnp.maximum(block, 0), shard, shard_count)
        begin = pl.multiple_of(place * HALF_TOKENS + core * share, share)
        for kind in range(2):
            base = (slot * 2 + kind) * share * 4
            for which in range(2):
                group = 2 * (pair if which == 0 else 1 - pair)
                wide[pl.ds(base + group + 1 - core, share, stride=4), :] = given_ref[
                    slot, kind, which
                ].astype(jnp.float32)
                for index in range(shard_count):

                    @pl.when((block >= 0) & (shift == index))
                    def _():
                        rows = (stay, cross)[which][index][kind, pl.ds(begin, share), :]
                        wide[pl.ds(base + group + core, share, stride=4), :] = rows.astype(
                            jnp.float32
                        )

                @pl.when(block < 0)
                def _():
                    wide[pl.ds(base + group + core, share, stride=4), :] = jnp.zeros(
                        (share, wide.shape[1]), jnp.float32
                    )

    out_ref[...] = wide[...].astype(jnp.bfloat16)


def place(order, partner, stay, cross, given, shard_count):
    smem = pl.BlockSpec(memory_space=pltpu.SMEM)
    vmem = pl.BlockSpec(memory_space=pltpu.VMEM)
    rows = CAP * 2 * (HALF_TOKENS // 2) * 4
    width = stay[0].shape[2]
    return pl.pallas_call(
        functools.partial(place_kernel, shard_count),
        out_shape=jax.ShapeDtypeStruct((rows, width), jnp.bfloat16),
        in_specs=[smem, smem] + [vmem] * (2 * shard_count + 1),
        out_specs=vmem,
        scratch_shapes=[pltpu.SMEM((CAP,), jnp.int32), pltpu.VMEM((rows, width), jnp.float32)],
        name="place_slots",
    )(order, partner, *stay, *cross, given)


def ring(array, step, count):
    return lax.ppermute(array, "ctx", [(i, (i + step) % count) for i in range(count)])


def swap(array, axis):
    return lax.ppermute(array, axis, [(0, 1), (1, 0)])


def pieces_program(queries, keys, values, span_order, lengths, kv_partner):
    count = lax.axis_size("ctx")
    query_rows, heads, width = queries.shape
    partner = kv_partner[:, 0]
    query = queries.reshape(query_rows * heads, width)
    keys_flat = keys.reshape(-1, width)
    values_flat = values.reshape(-1, width)
    cross0, stay0 = split_heads(
        keys_flat,
        swap(keys, "tp").reshape(-1, width),
        values_flat,
        swap(values, "tp").reshape(-1, width),
    )
    cross3 = ring(cross0, 1, count)
    cross1 = ring(cross0, -1, count)
    stay3 = ring(stay0, 1, count)
    cross2 = ring(cross3, 1, count)
    stay1 = ring(stay0, -1, count)
    stay2 = ring(stay1, -1, count)
    over = [swap(piece, "pair") for piece in (cross0, cross1, cross2, cross3)]
    state = None
    steps = (
        ((cross0, stay0), ((0, True), (0, False))),
        ((cross1, cross3, stay3), ((1, True), (3, True), (3, False))),
        ((cross2, stay1), ((2, True), (1, False))),
        ((stay2,), ((2, False),)),
    )
    for number, (pieces, sources) in enumerate(steps):
        last = number == len(steps) - 1
        state = attend(span_order, lengths, query, pieces, sources, state, last, count, heads)
    attended = state.reshape(queries.shape)
    stay = (stay0, stay1, stay2, stay3)
    given = swap(pick(span_order, partner, stay, over, count), "tp")
    cache = place(span_order, partner, stay, over, given, count)
    return attended, cache.reshape(CAP, 2, HALF_TOKENS // 2, 4, width)


def pick_program(mesh):
    sizes = mesh.shape
    fits = sizes["ctx"] == 4 and sizes["pair"] == 2 and sizes["tp"] == 2
    return pieces_program if fits else shards


def solution(mesh):
    return jax.shard_map(
        pick_program(mesh),
        mesh=mesh,
        in_specs=(
            P(("groups", "ctx"), ("pair", "tp"), None),
            P(("groups", "ctx", "tp"), "pair", None),
            P(("groups", "ctx", "tp"), "pair", None),
            P("groups"),
            P("groups"),
            P("groups", None),
        ),
        out_specs=(
            P(("groups", "ctx"), ("pair", "tp"), None),
            P(("groups", "ctx"), None, ("pair", "tp"), None, None),
        ),
        check_vma=False,
    )
```

```python
import functools

import jax
import jax.numpy as jnp
from jax import lax
from jax.experimental import pallas as pl
from jax.experimental.pallas import tpu as pltpu
from jax.sharding import PartitionSpec as P

GROUP = 4
BLK = 128
CAP = 8


neg_big = -1e30
key_block = 1024


def lookup(entries, where_at):
    entry_count = entries.shape[0]
    matches = where_at[..., None] == jnp.arange(entry_count, dtype=jnp.int32)
    return jnp.sum(jnp.where(matches, entries, 0), axis=-1)


def row_position(row_index, span_order, span_total, half_rows):
    block_index = row_index // half_rows
    leading = lookup(span_order, block_index // 2)
    span_index = jnp.where(block_index % 2 == 0, leading, span_total - 1 - leading)
    return span_index * half_rows + row_index % half_rows


def position_row(position, span_order, span_total, half_rows):
    span_index = position // half_rows
    shard_index = jnp.arange(span_order.shape[0], dtype=jnp.int32)
    even_match = span_order == span_index[..., None]
    odd_match = span_total - 1 - span_order == span_index[..., None]
    block_index = jnp.sum(
        jnp.where(even_match, 2 * shard_index, 0) + jnp.where(odd_match, 2 * shard_index + 1, 0),
        axis=-1,
    )
    return block_index * half_rows + position % half_rows


def request_of(position, lengths):
    boundary = jnp.cumsum(lengths)
    return jnp.sum((boundary <= position[..., None]).astype(jnp.int32), axis=-1)


def keep_state(inner):
    return inner


def shards(queries, keys, values, span_order, lengths, kv_partner):
    pair_count = lax.axis_size("pair")
    core_count = lax.axis_size("tp")
    span_total = 2 * lax.axis_size("ctx")
    ctx_index = lax.axis_index("ctx")
    core_index = lax.axis_index("tp")
    query_rows, local_heads, head_width = queries.shape
    half_rows = query_rows // 2
    local_groups = keys.shape[1]
    scale = head_width ** (-0.5)
    query_pos = row_position(
        ctx_index * query_rows + jnp.arange(query_rows, dtype=jnp.int32),
        span_order,
        span_total,
        half_rows,
    )
    query_req = request_of(query_pos, lengths)
    partner = kv_partner[:, 0]
    block_index = jnp.arange(partner.shape[0], dtype=jnp.int32)
    earlier = (partner[None, :] == partner[:, None]) & (block_index[None, :] < block_index[:, None])
    rank = jnp.sum(earlier.astype(jnp.int32), axis=1)
    slot_index = jnp.arange(CAP, dtype=jnp.int32)
    taken = (partner[None, :] == ctx_index) & (rank[None, :] == slot_index[:, None])
    slot_live = jnp.any(taken, axis=1)
    slot_block = jnp.sum(jnp.where(taken, block_index[None, :], 0), axis=1)
    token_share = BLK // (pair_count * core_count)
    pair_index = jnp.arange(pair_count, dtype=jnp.int32)

    def make_absorb(query_block, kv_pick, gathered_row, target, live):

        def attend(state, block_keys, block_values, key_rows):
            key_pos = row_position(key_rows, span_order, span_total, half_rows)
            key_req = request_of(key_pos, lengths)
            visible = (key_pos[None, :] <= query_pos[:, None]) & (
                key_req[None, :] == query_req[:, None]
            )

            def update(inner):
                peak, total, summed = inner
                head_keys = jnp.take(block_keys, kv_pick, axis=1)
                head_values = jnp.take(block_values, kv_pick, axis=1)
                scores = (
                    jnp.einsum(
                        "rhd,nhd->rhn", query_block, head_keys, preferred_element_type=jnp.float32
                    )
                    * scale
                )
                scores = jnp.where(visible[:, None, :], scores, neg_big)
                new_peak = jnp.maximum(peak, jnp.max(scores, axis=2))
                weights = jnp.where(
                    visible[:, None, :], jnp.exp(scores - new_peak[:, :, None]), 0.0
                )
                factor = jnp.exp(peak - new_peak)
                new_total = total * factor + jnp.sum(weights, axis=2)
                product = jnp.einsum(
                    "rhn,nhd->rhd",
                    weights.astype(jnp.bfloat16),
                    head_values,
                    preferred_element_type=jnp.float32,
                )
                return (new_peak, new_total, summed * factor[:, :, None] + product)

            return lax.cond(jnp.any(visible), update, keep_state, state)

        def absorb(carry, piece, start):
            state, selected = carry
            piece_keys, piece_values = piece
            count = piece_keys.shape[0]
            inside = live & (target >= 0) & (target < count)
            safe = jnp.clip(target, 0, count - 1)
            picked = jnp.stack(
                [jnp.take(piece_keys, safe, axis=0), jnp.take(piece_values, safe, axis=0)], axis=1
            )
            selected = jnp.where(
                inside[:, None, :, :, :, None, None], picked, jnp.zeros((), jnp.bfloat16)
            )
            turns = count // key_block
            shaped_keys = piece_keys.reshape(turns, key_block, local_groups, head_width)
            shaped_values = piece_values.reshape(turns, key_block, local_groups, head_width)
            block_starts = key_block * jnp.arange(turns, dtype=jnp.int32)

            def one_block(inner, items):
                block_keys, block_values, block_start = items
                key_rows = gathered_row(block_start + jnp.arange(key_block, dtype=jnp.int32))
                return (attend(inner, block_keys, block_values, key_rows), None)

            state, _ = lax.scan(one_block, state, (shaped_keys, shaped_values, block_starts))
            return (state, selected)

        return absorb

    def same_rows(row_index):
        return row_index

    kv_pick = (core_index * local_heads + jnp.arange(local_heads, dtype=jnp.int32)) // GROUP
    ranges = pair_index[:, None] * core_count + jnp.reshape(core_index, (1,))[None, :]
    wanted = (
        slot_block[:, None, None, None] * BLK
        + ranges[None, :, :, None] * token_share
        + jnp.arange(token_share, dtype=jnp.int32)[None, None, None, :]
    )
    target = position_row(wanted, span_order, span_total, half_rows)
    live = jnp.broadcast_to(slot_live[:, None, None, None], target.shape)
    absorb = make_absorb(queries, kv_pick, same_rows, target, live)
    state = (
        jnp.full((query_rows, local_heads), neg_big, jnp.float32),
        jnp.zeros((query_rows, local_heads), jnp.float32),
        jnp.zeros((query_rows, local_heads, head_width), jnp.float32),
    )
    selected = jnp.zeros(
        target.shape[:1] + (2,) + target.shape[1:] + (local_groups, head_width), jnp.bfloat16
    )
    (peak, total, summed), selected = absorb(
        (state, selected),
        (
            lax.all_gather(keys, ("ctx", "tp"), axis=0, tiled=True),
            lax.all_gather(values, ("ctx", "tp"), axis=0, tiled=True),
        ),
        jnp.int32(0),
    )
    selected = selected[:, :, :, 0]
    attended = (summed / total[:, :, None]).astype(jnp.bfloat16)
    received = lax.all_to_all(selected, "pair", split_axis=2, concat_axis=4, tiled=True)
    decode_cache = received.reshape(CAP, 2, token_share, pair_count * local_groups, head_width)
    return (attended, decode_cache)


HALF_TOKENS = BLK // 2
LOG2E = 1.4426950408889634
MASKED = -1e30
FLOOR = -1e29
COST_FLOPS = 4 * 10**9
Q_TILE = 1024
STRIP = 64


def split_kernel(key_a, key_b, value_a, value_b, cross_ref, stay_ref, wide):
    pair = lax.axis_index("pair")
    core = lax.axis_index("tp")
    for kind, (own, other) in enumerate(((key_a, key_b), (value_a, value_b))):
        wide[kind, core] = own[...].astype(jnp.float32)
        wide[kind, 1 - core] = other[...].astype(jnp.float32)
    for kind in range(2):
        for block in range(4):
            at = pl.ds(block * HALF_TOKENS, HALF_TOKENS)
            for out, part in ((cross_ref, 1 - pair), (stay_ref, pair)):
                first = (block % 2) * 2 * BLK + part * 2 * HALF_TOKENS + core
                rows = wide[kind, block // 2, pl.ds(first, HALF_TOKENS, stride=2), :]
                rows = rows.astype(jnp.bfloat16)
                out[kind, at, :] = rows


def split_heads(keys, keys_other, values, values_other):
    rows, width = keys.shape
    piece = jax.ShapeDtypeStruct((2, rows // 2, width), jnp.bfloat16)
    return pl.pallas_call(
        split_kernel,
        out_shape=(piece, piece),
        scratch_shapes=[pltpu.VMEM((2, 2, rows, width), jnp.float32)],
        name="split_heads",
    )(keys, keys_other, values, values_other)


def attend_kernel(sources, first, last, span_total, heads, *refs):
    order_ref, lengths_ref, query_ref = refs[:3]
    refs = refs[3:]
    pieces = []
    for _ in sources:
        pieces.append((refs[0], refs[1]))
        refs = refs[2:]
    if not first:
        peak_in, total_in, summed_in = refs[:3]
        refs = refs[3:]
    if last:
        out_ref, refs = refs[0], refs[1:]
    else:
        peak_out, total_out, summed_out = refs[:3]
        refs = refs[3:]
    score_ref, weights_ref, values_ref, top_ref, total_ref, summed_ref = refs
    shard = lax.axis_index("ctx")
    pair = lax.axis_index("pair")
    rows, width = query_ref.shape
    half_rows = rows // heads // 2
    factor = LOG2E * width**-0.5
    starts = [jnp.int32(0)]
    for r in range(lengths_ref.shape[0] - 1):
        starts.append(starts[-1] + lengths_ref[r])

    def begin_of(position):
        begin = jnp.zeros_like(position)
        for start in starts[1:]:
            begin = jnp.where(start <= position, start, begin)
        return begin

    spans = []
    for shift, (cross, stay) in zip(sources, pieces):
        lead = order_ref[lax.rem(shard + shift, span_total // 2)]
        spans.append((lead, cross, stay, 0))
        spans.append((span_total - 1 - lead, cross, stay, 1))
    part_keys = pieces[0][0].shape[1] // 2
    keys_each = 2 * part_keys
    for number, (_, cross, stay, half) in enumerate(spans):
        for which, piece in enumerate((cross, stay)):
            values_ref[number, pl.ds(which * part_keys, part_keys), :] = piece[
                1, pl.ds(half * part_keys, part_keys), :
            ]
    lane = lax.broadcasted_iota(jnp.int32, (1, keys_each), 1)
    in_part = lax.rem(lane, part_keys)
    local = (
        in_part
        + jnp.where(in_part >= HALF_TOKENS, BLK - HALF_TOKENS, 0)
        + HALF_TOKENS * jnp.where(lane < part_keys, 1 - pair, pair)
    )

    tile_tokens = Q_TILE // heads
    tiles_half = half_rows // tile_tokens

    def tile(index, _):
        at = pl.ds(pl.multiple_of(index * Q_TILE, Q_TILE), Q_TILE)
        own_lead = order_ref[shard]
        query_span = jnp.where(index < tiles_half, own_lead, span_total - 1 - own_lead)
        first_pos = query_span * half_rows + lax.rem(index, tiles_half) * tile_tokens
        begin_low = begin_of(first_pos)
        near = []
        for span, _, _, _ in spans:
            near.append(
                (span * half_rows <= first_pos + tile_tokens - 1)
                & (span * half_rows + half_rows - 1 >= begin_low)
            )
        if first:
            top_ref[...] = jnp.full(top_ref.shape, FLOOR, jnp.float32)
        else:
            top_ref[...] = peak_in[at, :]

        for number, (span, cross, stay, half) in enumerate(spans):

            @pl.when(near[number])
            def _():
                part = pl.ds(half * part_keys, part_keys)
                score_ref[number] = lax.dot_general(
                    query_ref[at, :],
                    jnp.concatenate([cross[0, part, :], stay[0, part, :]], axis=0),
                    (((1,), (1,)), ((), ())),
                    preferred_element_type=jnp.float32,
                )
                key_pos = span * half_rows + local
                for row in range(0, Q_TILE, STRIP):
                    strip = pl.ds(row, STRIP)
                    index_in = lax.broadcasted_iota(jnp.int32, (STRIP, width), 0)
                    query_pos = first_pos + row // heads + index_in // heads
                    query_begin = begin_of(query_pos)
                    top = top_ref[strip, :]
                    for column in range(0, keys_each, width):
                        at_key = key_pos[:, column : column + width]
                        visible = (at_key <= query_pos) & (at_key >= query_begin)
                        score = score_ref[number, strip, column : column + width]
                        score = jnp.where(visible, score, MASKED)
                        score_ref[number, strip, column : column + width] = score
                        top = jnp.maximum(top, score)
                    top_ref[strip, :] = top

        for row in range(0, Q_TILE, STRIP):
            strip = pl.ds(row, STRIP)
            peak = jnp.max(top_ref[strip, :], axis=1, keepdims=True)
            peak = jnp.broadcast_to(peak, (STRIP, width))
            top_ref[strip, :] = peak
            rows_at = pl.ds(pl.multiple_of(index * Q_TILE + row, STRIP), STRIP)
            if first:
                total_ref[strip, :] = jnp.zeros((STRIP, width), jnp.float32)
                summed_ref[strip, :] = jnp.zeros((STRIP, width), jnp.float32)
            else:
                fade = jnp.exp2((peak_in[rows_at, :] - peak) * factor)
                total_ref[strip, :] = total_in[rows_at, :] * fade
                summed_ref[strip, :] = summed_in[rows_at, :] * fade
            if not last:
                peak_out[rows_at, :] = peak
        for number in range(len(spans)):

            @pl.when(near[number])
            def _():
                for row in range(0, Q_TILE, STRIP):
                    strip = pl.ds(row, STRIP)
                    peak = top_ref[strip, :]
                    total = total_ref[strip, :]
                    for column in range(0, keys_each, width):
                        score = score_ref[number, strip, column : column + width]
                        weight = jnp.exp2((score - peak) * factor)
                        total = total + weight
                        weights_ref[strip, column : column + width] = weight.astype(jnp.bfloat16)
                    total_ref[strip, :] = total
                summed_ref[...] += jnp.dot(
                    weights_ref[...], values_ref[number], preferred_element_type=jnp.float32
                )

        if last:
            total = jnp.sum(total_ref[...], axis=1, keepdims=True)
            out_ref[at, :] = (summed_ref[...] / total).astype(jnp.bfloat16)
        else:
            total_out[at, :] = total_ref[...]
            summed_out[at, :] = summed_ref[...]
        return 0

    lax.fori_loop(0, rows // Q_TILE, tile, 0)


def attend(order, lengths, query, pieces, sources, state, last, heads):
    rows, width = query.shape
    first = state is None
    smem = pl.BlockSpec(memory_space=pltpu.SMEM)
    vmem = pl.BlockSpec(memory_space=pltpu.VMEM)
    state = () if first else state
    if last:
        out_shape = jax.ShapeDtypeStruct((rows, width), jnp.bfloat16)
        out_specs = vmem
    else:
        out_shape = (jax.ShapeDtypeStruct((rows, width), jnp.float32),) * 3
        out_specs = (vmem,) * 3
    keys_each = pieces[0].shape[-2]
    count = 2 * len(sources)
    tile = pltpu.VMEM((Q_TILE, width), jnp.float32)
    return pl.pallas_call(
        functools.partial(attend_kernel, sources, first, last, 2 * order.shape[0], heads),
        out_shape=out_shape,
        in_specs=[smem, smem] + [vmem] * (1 + len(pieces) + len(state)),
        out_specs=out_specs,
        scratch_shapes=[
            pltpu.VMEM((count, Q_TILE, keys_each), jnp.float32),
            pltpu.VMEM((Q_TILE, keys_each), jnp.bfloat16),
            pltpu.VMEM((count, keys_each, width), jnp.bfloat16),
            tile,
            tile,
            tile,
        ],
        cost_estimate=pl.CostEstimate(
            flops=COST_FLOPS, bytes_accessed=4 * rows * width, transcendentals=0
        ),
        name="attend",
    )(order, lengths, query, *pieces, *state)


def locate_slots(order_ref, partner_ref, found, shard, shard_count):
    for slot in range(CAP):
        found[0, slot] = -1
    for index in range(shard_count):
        lead = order_ref[index]
        shift = lax.rem(index - shard + shard_count, shard_count)
        found[1, lead] = shift
        found[2, lead] = 0
        found[1, 2 * shard_count - 1 - lead] = shift
        found[2, 2 * shard_count - 1 - lead] = 1
    taken = jnp.int32(0)
    for block in range(partner_ref.shape[0]):
        mine = partner_ref[block] == shard

        @pl.when(mine)
        def _():
            found[0, taken] = block

        taken = taken + mine.astype(jnp.int32)


def slot_place(found, slot):
    block = found[0, slot]
    span = jnp.maximum(block, 0) // 2
    place = found[2, span] * 2 + lax.rem(jnp.maximum(block, 0), 2)
    return block >= 0, found[1, span], place * HALF_TOKENS


def gather_pieces(pieces, count, held):
    for index, piece in enumerate(pieces):
        held[index // count, index % count] = piece[...]


def pick_kernel(order_ref, partner_ref, *refs):
    count = order_ref.shape[0]
    out_ref, found, held = refs[2 * count :]
    shard = lax.axis_index("ctx")
    core = lax.axis_index("tp")
    share = HALF_TOKENS // 2
    gather_pieces(refs[: 2 * count], count, held)
    locate_slots(order_ref, partner_ref, found, shard, count)
    for slot in range(CAP):
        live, index, start = slot_place(found, slot)
        begin = pl.ds(pl.multiple_of(start + (1 - core) * share, share), share)
        for which in range(2):
            for kind in range(2):
                out_ref[slot, kind, which] = held[which, index, kind, begin, :]


def slot_call(kernel, out_shape, scratch, name, operands, piece_shape):
    smem = pl.BlockSpec(memory_space=pltpu.SMEM)
    vmem = pl.BlockSpec(memory_space=pltpu.VMEM)
    count = operands[0].shape[0]
    return pl.pallas_call(
        kernel,
        out_shape=out_shape,
        in_specs=[smem, smem] + [vmem] * (len(operands) - 2),
        out_specs=vmem,
        scratch_shapes=[
            pltpu.SMEM((3, max(CAP, 2 * count)), jnp.int32),
            pltpu.VMEM((2, count) + piece_shape, jnp.bfloat16),
        ]
        + scratch,
        name=name,
    )(*operands)


def pick(order, partner, stay, cross):
    piece_shape = cross[0].shape
    out_shape = jax.ShapeDtypeStruct((CAP, 2, 2, HALF_TOKENS // 2, piece_shape[2]), jnp.bfloat16)
    operands = (order, partner, *stay, *cross)
    return slot_call(pick_kernel, out_shape, [], "pick_slots", operands, piece_shape)


def place_kernel(order_ref, partner_ref, *refs):
    count = order_ref.shape[0]
    given_ref, out_ref, found, held, wide = refs[2 * count :]
    shard = lax.axis_index("ctx")
    pair = lax.axis_index("pair")
    core = lax.axis_index("tp")
    share = HALF_TOKENS // 2
    gather_pieces(refs[: 2 * count], count, held)
    locate_slots(order_ref, partner_ref, found, shard, count)
    for slot in range(CAP):
        live, index, start = slot_place(found, slot)
        begin = pl.ds(pl.multiple_of(start + core * share, share), share)
        for which in range(2):
            group = 2 * (pair if which == 0 else 1 - pair)
            for kind in range(2):
                base = (slot * 2 + kind) * share * 4 + group
                kept = held[which, index, kind, begin, :].astype(jnp.float32)
                given = given_ref[slot, kind, which].astype(jnp.float32)
                wide[pl.ds(base + core, share, stride=4), :] = jnp.where(live, kept, 0.0)
                wide[pl.ds(base + 1 - core, share, stride=4), :] = jnp.where(live, given, 0.0)
    out_ref[...] = wide[...].astype(jnp.bfloat16)


def place(order, partner, stay, cross, given):
    piece_shape = cross[0].shape
    rows = CAP * 2 * (HALF_TOKENS // 2) * 4
    out_shape = jax.ShapeDtypeStruct((rows, piece_shape[2]), jnp.bfloat16)
    scratch = [pltpu.VMEM((rows, piece_shape[2]), jnp.float32)]
    operands = (order, partner, *stay, *cross, given)
    return slot_call(place_kernel, out_shape, scratch, "place_slots", operands, piece_shape)


def ring(array, step, count):
    return lax.ppermute(array, "ctx", [(i, (i + step) % count) for i in range(count)])


def swap(array, axis):
    return lax.ppermute(array, axis, [(0, 1), (1, 0)])


def after(value, earlier):
    return lax.optimization_barrier((value, earlier))


def pieces_program(queries, keys, values, span_order, lengths, kv_partner):
    count = lax.axis_size("ctx")
    query_rows, heads, width = queries.shape
    partner = kv_partner[:, 0]
    query = queries.reshape(query_rows * heads, width)
    cross0, stay0 = split_heads(
        keys.reshape(-1, width),
        swap(keys, "tp").reshape(-1, width),
        values.reshape(-1, width),
        swap(values, "tp").reshape(-1, width),
    )

    def step(pieces, sources, state, last=False):
        return attend(span_order, lengths, query, pieces, sources, state, last, heads)

    cross3 = ring(cross0, 1, count)
    cross1 = ring(cross0, -1, count)
    stay1 = ring(stay0, -1, count)
    stay3 = ring(stay0, 1, count)
    over0 = swap(cross0, "pair")
    cross2 = ring(cross3, 1, count)
    over3 = swap(cross3, "pair")
    over1 = swap(cross1, "pair")
    stay2 = ring(stay3, 1, count)
    stay0_late, stay3 = after(stay0, stay3)
    state = step((cross0, stay0_late, cross1, stay1), (0, 1), None)
    over2 = swap(cross2, "pair")
    attended = step((cross3, stay3, cross2, stay2), (3, 2), state, True)
    over2, attended = after(over2, attended)
    stay = (stay0, stay1, stay2, stay3)
    over = (over0, over1, over2, over3)
    given = swap(pick(span_order, partner, stay, over), "tp")
    cache = place(span_order, partner, stay, over, given)
    return attended.reshape(queries.shape), cache.reshape(CAP, 2, HALF_TOKENS // 2, 4, width)


def pick_program(mesh):
    sizes = mesh.shape
    fits = sizes["ctx"] == 4 and sizes["pair"] == 2 and sizes["tp"] == 2
    return pieces_program if fits else shards


def solution(mesh):
    return jax.shard_map(
        pick_program(mesh),
        mesh=mesh,
        in_specs=(
            P(("groups", "ctx"), ("pair", "tp"), None),
            P(("groups", "ctx", "tp"), "pair", None),
            P(("groups", "ctx", "tp"), "pair", None),
            P("groups"),
            P("groups"),
            P("groups", None),
        ),
        out_specs=(
            P(("groups", "ctx"), ("pair", "tp"), None),
            P(("groups", "ctx"), None, ("pair", "tp"), None, None),
        ),
        check_vma=False,
    )
```

```python
import functools

import jax
import jax.numpy as jnp
from jax import lax
from jax.experimental import pallas as pl
from jax.experimental.pallas import tpu as pltpu
from jax.sharding import PartitionSpec as P

GROUP = 4
BLK = 128
CAP = 8


neg_big = -1e30
key_block = 1024


def lookup(entries, where_at):
    entry_count = entries.shape[0]
    matches = where_at[..., None] == jnp.arange(entry_count, dtype=jnp.int32)
    return jnp.sum(jnp.where(matches, entries, 0), axis=-1)


def row_position(row_index, span_order, span_total, half_rows):
    block_index = row_index // half_rows
    leading = lookup(span_order, block_index // 2)
    span_index = jnp.where(block_index % 2 == 0, leading, span_total - 1 - leading)
    return span_index * half_rows + row_index % half_rows


def position_row(position, span_order, span_total, half_rows):
    span_index = position // half_rows
    shard_index = jnp.arange(span_order.shape[0], dtype=jnp.int32)
    even_match = span_order == span_index[..., None]
    odd_match = span_total - 1 - span_order == span_index[..., None]
    block_index = jnp.sum(
        jnp.where(even_match, 2 * shard_index, 0) + jnp.where(odd_match, 2 * shard_index + 1, 0),
        axis=-1,
    )
    return block_index * half_rows + position % half_rows


def request_of(position, lengths):
    boundary = jnp.cumsum(lengths)
    return jnp.sum((boundary <= position[..., None]).astype(jnp.int32), axis=-1)


def keep_state(inner):
    return inner


def shards(queries, keys, values, span_order, lengths, kv_partner):
    pair_count = lax.axis_size("pair")
    core_count = lax.axis_size("tp")
    span_total = 2 * lax.axis_size("ctx")
    ctx_index = lax.axis_index("ctx")
    core_index = lax.axis_index("tp")
    query_rows, local_heads, head_width = queries.shape
    half_rows = query_rows // 2
    local_groups = keys.shape[1]
    scale = head_width ** (-0.5)
    query_pos = row_position(
        ctx_index * query_rows + jnp.arange(query_rows, dtype=jnp.int32),
        span_order,
        span_total,
        half_rows,
    )
    query_req = request_of(query_pos, lengths)
    partner = kv_partner[:, 0]
    block_index = jnp.arange(partner.shape[0], dtype=jnp.int32)
    earlier = (partner[None, :] == partner[:, None]) & (block_index[None, :] < block_index[:, None])
    rank = jnp.sum(earlier.astype(jnp.int32), axis=1)
    slot_index = jnp.arange(CAP, dtype=jnp.int32)
    taken = (partner[None, :] == ctx_index) & (rank[None, :] == slot_index[:, None])
    slot_live = jnp.any(taken, axis=1)
    slot_block = jnp.sum(jnp.where(taken, block_index[None, :], 0), axis=1)
    token_share = BLK // (pair_count * core_count)
    pair_index = jnp.arange(pair_count, dtype=jnp.int32)

    def make_absorb(query_block, kv_pick, gathered_row, target, live):

        def attend(state, block_keys, block_values, key_rows):
            key_pos = row_position(key_rows, span_order, span_total, half_rows)
            key_req = request_of(key_pos, lengths)
            visible = (key_pos[None, :] <= query_pos[:, None]) & (
                key_req[None, :] == query_req[:, None]
            )

            def update(inner):
                peak, total, summed = inner
                head_keys = jnp.take(block_keys, kv_pick, axis=1)
                head_values = jnp.take(block_values, kv_pick, axis=1)
                scores = (
                    jnp.einsum(
                        "rhd,nhd->rhn", query_block, head_keys, preferred_element_type=jnp.float32
                    )
                    * scale
                )
                scores = jnp.where(visible[:, None, :], scores, neg_big)
                new_peak = jnp.maximum(peak, jnp.max(scores, axis=2))
                weights = jnp.where(
                    visible[:, None, :], jnp.exp(scores - new_peak[:, :, None]), 0.0
                )
                factor = jnp.exp(peak - new_peak)
                new_total = total * factor + jnp.sum(weights, axis=2)
                product = jnp.einsum(
                    "rhn,nhd->rhd",
                    weights.astype(jnp.bfloat16),
                    head_values,
                    preferred_element_type=jnp.float32,
                )
                return (new_peak, new_total, summed * factor[:, :, None] + product)

            return lax.cond(jnp.any(visible), update, keep_state, state)

        def absorb(carry, piece, start):
            state, selected = carry
            piece_keys, piece_values = piece
            count = piece_keys.shape[0]
            inside = live & (target >= 0) & (target < count)
            safe = jnp.clip(target, 0, count - 1)
            picked = jnp.stack(
                [jnp.take(piece_keys, safe, axis=0), jnp.take(piece_values, safe, axis=0)], axis=1
            )
            selected = jnp.where(
                inside[:, None, :, :, :, None, None], picked, jnp.zeros((), jnp.bfloat16)
            )
            turns = count // key_block
            shaped_keys = piece_keys.reshape(turns, key_block, local_groups, head_width)
            shaped_values = piece_values.reshape(turns, key_block, local_groups, head_width)
            block_starts = key_block * jnp.arange(turns, dtype=jnp.int32)

            def one_block(inner, items):
                block_keys, block_values, block_start = items
                key_rows = gathered_row(block_start + jnp.arange(key_block, dtype=jnp.int32))
                return (attend(inner, block_keys, block_values, key_rows), None)

            state, _ = lax.scan(one_block, state, (shaped_keys, shaped_values, block_starts))
            return (state, selected)

        return absorb

    def same_rows(row_index):
        return row_index

    kv_pick = (core_index * local_heads + jnp.arange(local_heads, dtype=jnp.int32)) // GROUP
    ranges = pair_index[:, None] * core_count + jnp.reshape(core_index, (1,))[None, :]
    wanted = (
        slot_block[:, None, None, None] * BLK
        + ranges[None, :, :, None] * token_share
        + jnp.arange(token_share, dtype=jnp.int32)[None, None, None, :]
    )
    target = position_row(wanted, span_order, span_total, half_rows)
    live = jnp.broadcast_to(slot_live[:, None, None, None], target.shape)
    absorb = make_absorb(queries, kv_pick, same_rows, target, live)
    state = (
        jnp.full((query_rows, local_heads), neg_big, jnp.float32),
        jnp.zeros((query_rows, local_heads), jnp.float32),
        jnp.zeros((query_rows, local_heads, head_width), jnp.float32),
    )
    selected = jnp.zeros(
        target.shape[:1] + (2,) + target.shape[1:] + (local_groups, head_width), jnp.bfloat16
    )
    (peak, total, summed), selected = absorb(
        (state, selected),
        (
            lax.all_gather(keys, ("ctx", "tp"), axis=0, tiled=True),
            lax.all_gather(values, ("ctx", "tp"), axis=0, tiled=True),
        ),
        jnp.int32(0),
    )
    selected = selected[:, :, :, 0]
    attended = (summed / total[:, :, None]).astype(jnp.bfloat16)
    received = lax.all_to_all(selected, "pair", split_axis=2, concat_axis=4, tiled=True)
    decode_cache = received.reshape(CAP, 2, token_share, pair_count * local_groups, head_width)
    return (attended, decode_cache)


HALF_TOKENS = BLK // 2
LOG2E = 1.4426950408889634
MASKED = -1e30
FLOOR = -1e29
COST_FLOPS = 4 * 10**9
Q_TILE = 1024
STRIP = 64


def split_kernel(key_a, key_b, value_a, value_b, cross_ref, stay_ref, wide):
    pair = lax.axis_index("pair")
    core = lax.axis_index("tp")
    for kind, (own, other) in enumerate(((key_a, key_b), (value_a, value_b))):
        wide[kind, core] = own[...].astype(jnp.float32)
        wide[kind, 1 - core] = other[...].astype(jnp.float32)
    for kind in range(2):
        for block in range(4):
            at = pl.ds(block * HALF_TOKENS, HALF_TOKENS)
            for out, part in ((cross_ref, 1 - pair), (stay_ref, pair)):
                first = (block % 2) * 2 * BLK + part * 2 * HALF_TOKENS + core
                rows = wide[kind, block // 2, pl.ds(first, HALF_TOKENS, stride=2), :]
                rows = rows.astype(jnp.bfloat16)
                out[kind, at, :] = rows


def split_heads(keys, keys_other, values, values_other):
    rows, width = keys.shape
    piece = jax.ShapeDtypeStruct((2, rows // 2, width), jnp.bfloat16)
    return pl.pallas_call(
        split_kernel,
        out_shape=(piece, piece),
        scratch_shapes=[pltpu.VMEM((2, 2, rows, width), jnp.float32)],
        compiler_params=pltpu.CompilerParams(vmem_limit_bytes=12 * 2**20),
        name="split_heads",
    )(keys, keys_other, values, values_other)


def attend_kernel(sources, first, last, span_total, heads, *refs):
    order_ref, lengths_ref, query_ref = refs[:3]
    refs = refs[3:]
    pieces = []
    for _ in sources:
        pieces.append((refs[0], refs[1]))
        refs = refs[2:]
    if not first:
        peak_in, total_in, summed_in = refs[:3]
        refs = refs[3:]
    if last:
        out_ref, refs = refs[0], refs[1:]
    else:
        peak_out, total_out, summed_out = refs[:3]
        refs = refs[3:]
    score_ref, weights_ref, values_ref, top_ref, total_ref, summed_ref = refs
    shard = lax.axis_index("ctx")
    pair = lax.axis_index("pair")
    rows, width = query_ref.shape
    half_rows = rows // heads // 2
    factor = LOG2E * width**-0.5
    starts = [jnp.int32(0)]
    for r in range(lengths_ref.shape[0] - 1):
        starts.append(starts[-1] + lengths_ref[r])

    def begin_of(position):
        begin = jnp.zeros_like(position)
        for start in starts[1:]:
            begin = jnp.where(start <= position, start, begin)
        return begin

    spans = []
    for shift, (cross, stay) in zip(sources, pieces):
        lead = order_ref[lax.rem(shard + shift, span_total // 2)]
        spans.append((lead, cross, stay, 0))
        spans.append((span_total - 1 - lead, cross, stay, 1))
    part_keys = pieces[0][0].shape[1] // 2
    keys_each = 2 * part_keys
    for number, (_, cross, stay, half) in enumerate(spans):
        for which, piece in enumerate((cross, stay)):
            values_ref[number, pl.ds(which * part_keys, part_keys), :] = piece[
                1, pl.ds(half * part_keys, part_keys), :
            ]
    lane = lax.broadcasted_iota(jnp.int32, (1, keys_each), 1)
    in_part = lax.rem(lane, part_keys)
    local = (
        in_part
        + jnp.where(in_part >= HALF_TOKENS, BLK - HALF_TOKENS, 0)
        + HALF_TOKENS * jnp.where(lane < part_keys, 1 - pair, pair)
    )

    tile_tokens = Q_TILE // heads
    tiles_half = half_rows // tile_tokens

    def tile(index, _):
        at = pl.ds(pl.multiple_of(index * Q_TILE, Q_TILE), Q_TILE)
        own_lead = order_ref[shard]
        query_span = jnp.where(index < tiles_half, own_lead, span_total - 1 - own_lead)
        first_pos = query_span * half_rows + lax.rem(index, tiles_half) * tile_tokens
        begin_low = begin_of(first_pos)
        near = []
        for span, _, _, _ in spans:
            near.append(
                (span * half_rows <= first_pos + tile_tokens - 1)
                & (span * half_rows + half_rows - 1 >= begin_low)
            )
        if first:
            top_ref[...] = jnp.full(top_ref.shape, FLOOR, jnp.float32)
        else:
            top_ref[...] = peak_in[at, :]

        for number, (span, cross, stay, half) in enumerate(spans):

            @pl.when(near[number])
            def _():
                part = pl.ds(half * part_keys, part_keys)
                score_ref[number] = lax.dot_general(
                    query_ref[at, :],
                    jnp.concatenate([cross[0, part, :], stay[0, part, :]], axis=0),
                    (((1,), (1,)), ((), ())),
                    preferred_element_type=jnp.float32,
                )
                key_pos = span * half_rows + local
                for row in range(0, Q_TILE, STRIP):
                    strip = pl.ds(row, STRIP)
                    index_in = lax.broadcasted_iota(jnp.int32, (STRIP, width), 0)
                    query_pos = first_pos + row // heads + index_in // heads
                    query_begin = begin_of(query_pos)
                    top = top_ref[strip, :]
                    for column in range(0, keys_each, width):
                        at_key = key_pos[:, column : column + width]
                        visible = (at_key <= query_pos) & (at_key >= query_begin)
                        score = score_ref[number, strip, column : column + width]
                        score = jnp.where(visible, score, MASKED)
                        score_ref[number, strip, column : column + width] = score
                        top = jnp.maximum(top, score)
                    top_ref[strip, :] = top

        for row in range(0, Q_TILE, STRIP):
            strip = pl.ds(row, STRIP)
            peak = jnp.max(top_ref[strip, :], axis=1, keepdims=True)
            peak = jnp.broadcast_to(peak, (STRIP, width))
            top_ref[strip, :] = peak
            rows_at = pl.ds(pl.multiple_of(index * Q_TILE + row, STRIP), STRIP)
            if first:
                total_ref[strip, :] = jnp.zeros((STRIP, width), jnp.float32)
                summed_ref[strip, :] = jnp.zeros((STRIP, width), jnp.float32)
            else:
                fade = jnp.exp2((peak_in[rows_at, :] - peak) * factor)
                total_ref[strip, :] = total_in[rows_at, :] * fade
                summed_ref[strip, :] = summed_in[rows_at, :] * fade
            if not last:
                peak_out[rows_at, :] = peak
        for number in range(len(spans)):

            @pl.when(near[number])
            def _():
                for row in range(0, Q_TILE, STRIP):
                    strip = pl.ds(row, STRIP)
                    peak = top_ref[strip, :]
                    total = total_ref[strip, :]
                    for column in range(0, keys_each, width):
                        score = score_ref[number, strip, column : column + width]
                        weight = jnp.exp2((score - peak) * factor)
                        total = total + weight
                        weights_ref[strip, column : column + width] = weight.astype(jnp.bfloat16)
                    total_ref[strip, :] = total
                summed_ref[...] += jnp.dot(
                    weights_ref[...], values_ref[number], preferred_element_type=jnp.float32
                )

        if last:
            total = jnp.sum(total_ref[...], axis=1, keepdims=True)
            out_ref[at, :] = (summed_ref[...] / total).astype(jnp.bfloat16)
        else:
            total_out[at, :] = total_ref[...]
            summed_out[at, :] = summed_ref[...]
        return 0

    lax.fori_loop(0, rows // Q_TILE, tile, 0)


def attend(order, lengths, query, pieces, sources, state, last, heads):
    rows, width = query.shape
    first = state is None
    smem = pl.BlockSpec(memory_space=pltpu.SMEM)
    vmem = pl.BlockSpec(memory_space=pltpu.VMEM)
    state = () if first else state
    if last:
        out_shape = jax.ShapeDtypeStruct((rows, width), jnp.bfloat16)
        out_specs = vmem
    else:
        out_shape = (jax.ShapeDtypeStruct((rows, width), jnp.float32),) * 3
        out_specs = (vmem,) * 3
    keys_each = pieces[0].shape[-2]
    count = 2 * len(sources)
    tile = pltpu.VMEM((Q_TILE, width), jnp.float32)
    return pl.pallas_call(
        functools.partial(attend_kernel, sources, first, last, 2 * order.shape[0], heads),
        out_shape=out_shape,
        in_specs=[smem, smem] + [vmem] * (1 + len(pieces) + len(state)),
        out_specs=out_specs,
        scratch_shapes=[
            pltpu.VMEM((count, Q_TILE, keys_each), jnp.float32),
            pltpu.VMEM((Q_TILE, keys_each), jnp.bfloat16),
            pltpu.VMEM((count, keys_each, width), jnp.bfloat16),
            tile,
            tile,
            tile,
        ],
        cost_estimate=pl.CostEstimate(
            flops=COST_FLOPS, bytes_accessed=4 * rows * width, transcendentals=0
        ),
        compiler_params=pltpu.CompilerParams(vmem_limit_bytes=24 * 2**20),
        name="attend",
    )(order, lengths, query, *pieces, *state)


def locate_slots(order_ref, partner_ref, found, shard, shard_count):
    for slot in range(CAP):
        found[0, slot] = -1
    for index in range(shard_count):
        lead = order_ref[index]
        shift = lax.rem(index - shard + shard_count, shard_count)
        found[1, lead] = shift
        found[2, lead] = 0
        found[1, 2 * shard_count - 1 - lead] = shift
        found[2, 2 * shard_count - 1 - lead] = 1
    taken = jnp.int32(0)
    for block in range(partner_ref.shape[0]):
        mine = partner_ref[block] == shard

        @pl.when(mine)
        def _():
            found[0, taken] = block

        taken = taken + mine.astype(jnp.int32)


def slot_place(found, slot):
    block = found[0, slot]
    span = jnp.maximum(block, 0) // 2
    place = found[2, span] * 2 + lax.rem(jnp.maximum(block, 0), 2)
    return block >= 0, found[1, span], place * HALF_TOKENS


def gather_pieces(pieces, count, held):
    for index, piece in enumerate(pieces):
        held[index // count, index % count] = piece[...]


def pick_kernel(order_ref, partner_ref, *refs):
    count = order_ref.shape[0]
    out_ref, found, held = refs[2 * count :]
    shard = lax.axis_index("ctx")
    core = lax.axis_index("tp")
    share = HALF_TOKENS // 2
    gather_pieces(refs[: 2 * count], count, held)
    locate_slots(order_ref, partner_ref, found, shard, count)
    for slot in range(CAP):
        live, index, start = slot_place(found, slot)
        begin = pl.ds(pl.multiple_of(start + (1 - core) * share, share), share)
        for which in range(2):
            for kind in range(2):
                out_ref[slot, kind, which] = held[which, index, kind, begin, :]


def slot_call(kernel, out_shape, scratch, name, operands, piece_shape):
    smem = pl.BlockSpec(memory_space=pltpu.SMEM)
    vmem = pl.BlockSpec(memory_space=pltpu.VMEM)
    count = operands[0].shape[0]
    return pl.pallas_call(
        kernel,
        out_shape=out_shape,
        in_specs=[smem, smem] + [vmem] * (len(operands) - 2),
        out_specs=vmem,
        scratch_shapes=[
            pltpu.SMEM((3, max(CAP, 2 * count)), jnp.int32),
            pltpu.VMEM((2, count) + piece_shape, jnp.bfloat16),
        ]
        + scratch,
        compiler_params=pltpu.CompilerParams(vmem_limit_bytes=12 * 2**20),
        name=name,
    )(*operands)


def pick(order, partner, stay, cross):
    piece_shape = cross[0].shape
    out_shape = jax.ShapeDtypeStruct((CAP, 2, 2, HALF_TOKENS // 2, piece_shape[2]), jnp.bfloat16)
    operands = (order, partner, *stay, *cross)
    return slot_call(pick_kernel, out_shape, [], "pick_slots", operands, piece_shape)


def place_kernel(order_ref, partner_ref, *refs):
    count = order_ref.shape[0]
    given_ref, out_ref, found, held, wide = refs[2 * count :]
    shard = lax.axis_index("ctx")
    pair = lax.axis_index("pair")
    core = lax.axis_index("tp")
    share = HALF_TOKENS // 2
    gather_pieces(refs[: 2 * count], count, held)
    locate_slots(order_ref, partner_ref, found, shard, count)
    for slot in range(CAP):
        live, index, start = slot_place(found, slot)
        begin = pl.ds(pl.multiple_of(start + core * share, share), share)
        for which in range(2):
            group = 2 * (pair if which == 0 else 1 - pair)
            for kind in range(2):
                base = (slot * 2 + kind) * share * 4 + group
                kept = held[which, index, kind, begin, :].astype(jnp.float32)
                given = given_ref[slot, kind, which].astype(jnp.float32)
                wide[pl.ds(base + core, share, stride=4), :] = jnp.where(live, kept, 0.0)
                wide[pl.ds(base + 1 - core, share, stride=4), :] = jnp.where(live, given, 0.0)
    out_ref[...] = wide[...].astype(jnp.bfloat16)


def place(order, partner, stay, cross, given):
    piece_shape = cross[0].shape
    rows = CAP * 2 * (HALF_TOKENS // 2) * 4
    out_shape = jax.ShapeDtypeStruct((rows, piece_shape[2]), jnp.bfloat16)
    scratch = [pltpu.VMEM((rows, piece_shape[2]), jnp.float32)]
    operands = (order, partner, *stay, *cross, given)
    return slot_call(place_kernel, out_shape, scratch, "place_slots", operands, piece_shape)


def ring(array, step, count):
    return lax.ppermute(array, "ctx", [(i, (i + step) % count) for i in range(count)])


def swap(array, axis):
    return lax.ppermute(array, axis, [(0, 1), (1, 0)])


def after(value, earlier):
    return lax.optimization_barrier((value, earlier))


def pieces_program(queries, keys, values, span_order, lengths, kv_partner):
    count = lax.axis_size("ctx")
    query_rows, heads, width = queries.shape
    partner = kv_partner[:, 0]
    query = queries.reshape(query_rows * heads, width)
    cross0, stay0 = split_heads(
        keys.reshape(-1, width),
        swap(keys, "tp").reshape(-1, width),
        values.reshape(-1, width),
        swap(values, "tp").reshape(-1, width),
    )

    def step(pieces, sources, state, last=False):
        return attend(span_order, lengths, query, pieces, sources, state, last, heads)

    cross3 = ring(cross0, 1, count)
    cross1 = ring(cross0, -1, count)
    stay1 = ring(stay0, -1, count)
    stay3 = ring(stay0, 1, count)
    over0 = swap(cross0, "pair")
    cross2 = ring(cross3, 1, count)
    over3 = swap(cross3, "pair")
    over1 = swap(cross1, "pair")
    stay2 = ring(stay3, 1, count)
    stay0_late, stay3 = after(stay0, stay3)
    state = step((cross0, stay0_late, cross1, stay1), (0, 1), None)
    over2 = swap(cross2, "pair")
    attended = step((cross3, stay3, cross2, stay2), (3, 2), state, True)
    over2, attended = after(over2, attended)
    stay = (stay0, stay1, stay2, stay3)
    over = (over0, over1, over2, over3)
    given = swap(pick(span_order, partner, stay, over), "tp")
    cache = place(span_order, partner, stay, over, given)
    return attended.reshape(queries.shape), cache.reshape(CAP, 2, HALF_TOKENS // 2, 4, width)


def pick_program(mesh):
    sizes = mesh.shape
    fits = sizes["ctx"] == 4 and sizes["pair"] == 2 and sizes["tp"] == 2
    return pieces_program if fits else shards


def solution(mesh):
    return jax.shard_map(
        pick_program(mesh),
        mesh=mesh,
        in_specs=(
            P(("groups", "ctx"), ("pair", "tp"), None),
            P(("groups", "ctx", "tp"), "pair", None),
            P(("groups", "ctx", "tp"), "pair", None),
            P("groups"),
            P("groups"),
            P("groups", None),
        ),
        out_specs=(
            P(("groups", "ctx"), ("pair", "tp"), None),
            P(("groups", "ctx"), None, ("pair", "tp"), None, None),
        ),
        check_vma=False,
    )
```

```python
import functools

import jax
import jax.numpy as jnp
from jax import lax
from jax.experimental import pallas as pl
from jax.experimental.pallas import tpu as pltpu
from jax.sharding import PartitionSpec as P

GROUP = 4
BLK = 128
CAP = 8


neg_big = -1e30
key_block = 1024


def lookup(entries, where_at):
    entry_count = entries.shape[0]
    matches = where_at[..., None] == jnp.arange(entry_count, dtype=jnp.int32)
    return jnp.sum(jnp.where(matches, entries, 0), axis=-1)


def row_position(row_index, span_order, span_total, half_rows):
    block_index = row_index // half_rows
    leading = lookup(span_order, block_index // 2)
    span_index = jnp.where(block_index % 2 == 0, leading, span_total - 1 - leading)
    return span_index * half_rows + row_index % half_rows


def position_row(position, span_order, span_total, half_rows):
    span_index = position // half_rows
    shard_index = jnp.arange(span_order.shape[0], dtype=jnp.int32)
    even_match = span_order == span_index[..., None]
    odd_match = span_total - 1 - span_order == span_index[..., None]
    block_index = jnp.sum(
        jnp.where(even_match, 2 * shard_index, 0) + jnp.where(odd_match, 2 * shard_index + 1, 0),
        axis=-1,
    )
    return block_index * half_rows + position % half_rows


def request_of(position, lengths):
    boundary = jnp.cumsum(lengths)
    return jnp.sum((boundary <= position[..., None]).astype(jnp.int32), axis=-1)


def keep_state(inner):
    return inner


def shards(queries, keys, values, span_order, lengths, kv_partner):
    pair_count = lax.axis_size("pair")
    core_count = lax.axis_size("tp")
    span_total = 2 * lax.axis_size("ctx")
    ctx_index = lax.axis_index("ctx")
    core_index = lax.axis_index("tp")
    query_rows, local_heads, head_width = queries.shape
    half_rows = query_rows // 2
    local_groups = keys.shape[1]
    scale = head_width ** (-0.5)
    query_pos = row_position(
        ctx_index * query_rows + jnp.arange(query_rows, dtype=jnp.int32),
        span_order,
        span_total,
        half_rows,
    )
    query_req = request_of(query_pos, lengths)
    partner = kv_partner[:, 0]
    block_index = jnp.arange(partner.shape[0], dtype=jnp.int32)
    earlier = (partner[None, :] == partner[:, None]) & (block_index[None, :] < block_index[:, None])
    rank = jnp.sum(earlier.astype(jnp.int32), axis=1)
    slot_index = jnp.arange(CAP, dtype=jnp.int32)
    taken = (partner[None, :] == ctx_index) & (rank[None, :] == slot_index[:, None])
    slot_live = jnp.any(taken, axis=1)
    slot_block = jnp.sum(jnp.where(taken, block_index[None, :], 0), axis=1)
    token_share = BLK // (pair_count * core_count)
    pair_index = jnp.arange(pair_count, dtype=jnp.int32)

    def make_absorb(query_block, kv_pick, gathered_row, target, live):

        def attend(state, block_keys, block_values, key_rows):
            key_pos = row_position(key_rows, span_order, span_total, half_rows)
            key_req = request_of(key_pos, lengths)
            visible = (key_pos[None, :] <= query_pos[:, None]) & (
                key_req[None, :] == query_req[:, None]
            )

            def update(inner):
                peak, total, summed = inner
                head_keys = jnp.take(block_keys, kv_pick, axis=1)
                head_values = jnp.take(block_values, kv_pick, axis=1)
                scores = (
                    jnp.einsum(
                        "rhd,nhd->rhn", query_block, head_keys, preferred_element_type=jnp.float32
                    )
                    * scale
                )
                scores = jnp.where(visible[:, None, :], scores, neg_big)
                new_peak = jnp.maximum(peak, jnp.max(scores, axis=2))
                weights = jnp.where(
                    visible[:, None, :], jnp.exp(scores - new_peak[:, :, None]), 0.0
                )
                factor = jnp.exp(peak - new_peak)
                new_total = total * factor + jnp.sum(weights, axis=2)
                product = jnp.einsum(
                    "rhn,nhd->rhd",
                    weights.astype(jnp.bfloat16),
                    head_values,
                    preferred_element_type=jnp.float32,
                )
                return (new_peak, new_total, summed * factor[:, :, None] + product)

            return lax.cond(jnp.any(visible), update, keep_state, state)

        def absorb(carry, piece, start):
            state, selected = carry
            piece_keys, piece_values = piece
            count = piece_keys.shape[0]
            inside = live & (target >= 0) & (target < count)
            safe = jnp.clip(target, 0, count - 1)
            picked = jnp.stack(
                [jnp.take(piece_keys, safe, axis=0), jnp.take(piece_values, safe, axis=0)], axis=1
            )
            selected = jnp.where(
                inside[:, None, :, :, :, None, None], picked, jnp.zeros((), jnp.bfloat16)
            )
            turns = count // key_block
            shaped_keys = piece_keys.reshape(turns, key_block, local_groups, head_width)
            shaped_values = piece_values.reshape(turns, key_block, local_groups, head_width)
            block_starts = key_block * jnp.arange(turns, dtype=jnp.int32)

            def one_block(inner, items):
                block_keys, block_values, block_start = items
                key_rows = gathered_row(block_start + jnp.arange(key_block, dtype=jnp.int32))
                return (attend(inner, block_keys, block_values, key_rows), None)

            state, _ = lax.scan(one_block, state, (shaped_keys, shaped_values, block_starts))
            return (state, selected)

        return absorb

    def same_rows(row_index):
        return row_index

    kv_pick = (core_index * local_heads + jnp.arange(local_heads, dtype=jnp.int32)) // GROUP
    ranges = pair_index[:, None] * core_count + jnp.reshape(core_index, (1,))[None, :]
    wanted = (
        slot_block[:, None, None, None] * BLK
        + ranges[None, :, :, None] * token_share
        + jnp.arange(token_share, dtype=jnp.int32)[None, None, None, :]
    )
    target = position_row(wanted, span_order, span_total, half_rows)
    live = jnp.broadcast_to(slot_live[:, None, None, None], target.shape)
    absorb = make_absorb(queries, kv_pick, same_rows, target, live)
    state = (
        jnp.full((query_rows, local_heads), neg_big, jnp.float32),
        jnp.zeros((query_rows, local_heads), jnp.float32),
        jnp.zeros((query_rows, local_heads, head_width), jnp.float32),
    )
    selected = jnp.zeros(
        target.shape[:1] + (2,) + target.shape[1:] + (local_groups, head_width), jnp.bfloat16
    )
    (peak, total, summed), selected = absorb(
        (state, selected),
        (
            lax.all_gather(keys, ("ctx", "tp"), axis=0, tiled=True),
            lax.all_gather(values, ("ctx", "tp"), axis=0, tiled=True),
        ),
        jnp.int32(0),
    )
    selected = selected[:, :, :, 0]
    attended = (summed / total[:, :, None]).astype(jnp.bfloat16)
    received = lax.all_to_all(selected, "pair", split_axis=2, concat_axis=4, tiled=True)
    decode_cache = received.reshape(CAP, 2, token_share, pair_count * local_groups, head_width)
    return (attended, decode_cache)


HALF_TOKENS = BLK // 2
LOG2E = 1.4426950408889634
MASKED = -1e30
FLOOR = -1e29
COST_FLOPS = 4 * 10**9
Q_TILE = 1024
STRIP = 64


def find_kernel(order_ref, partner_ref, found_ref):
    locate_slots(order_ref, partner_ref, found_ref, lax.axis_index("ctx"), order_ref.shape[0])


def find(order, partner):
    smem = pl.BlockSpec(memory_space=pltpu.SMEM)
    return pl.pallas_call(
        find_kernel,
        out_shape=jax.ShapeDtypeStruct((3, max(CAP, 2 * order.shape[0])), jnp.int32),
        in_specs=[smem, smem],
        out_specs=smem,
        compiler_params=pltpu.CompilerParams(vmem_limit_bytes=8 * 2**20),
        name="find_slots",
    )(order, partner)


def split_kernel(cross, own_ref, key_other, value_other, out_ref, wide):
    pair = lax.axis_index("pair")
    core = lax.axis_index("tp")
    part = 1 - pair if cross else pair
    for kind, other in enumerate((key_other, value_other)):
        wide[kind, core] = own_ref[kind]
        wide[kind, 1 - core] = other[...].astype(jnp.float32)
    for kind in range(2):
        for block in range(4):
            first = (block % 2) * 2 * BLK + part * 2 * HALF_TOKENS + core
            rows = wide[kind, block // 2, pl.ds(first, HALF_TOKENS, stride=2), :]
            out_ref[kind, pl.ds(block * HALF_TOKENS, HALF_TOKENS), :] = rows.astype(jnp.bfloat16)


def split_heads(own, keys_other, values_other, cross):
    _, rows, width = own.shape
    return pl.pallas_call(
        functools.partial(split_kernel, cross),
        out_shape=jax.ShapeDtypeStruct((2, rows // 2, width), jnp.bfloat16),
        scratch_shapes=[pltpu.VMEM((2, 2, rows, width), jnp.float32)],
        compiler_params=pltpu.CompilerParams(vmem_limit_bytes=12 * 2**20),
        name="split_heads",
    )(own, keys_other, values_other)


def attend_kernel(sources, first, last, span_total, heads, *refs):
    order_ref, lengths_ref, query_ref = refs[:3]
    refs = refs[3:]
    pieces = []
    for _ in sources:
        pieces.append((refs[0], refs[1]))
        refs = refs[2:]
    if not first:
        peak_in, total_in, summed_in = refs[:3]
        refs = refs[3:]
    if last:
        out_ref, refs = refs[0], refs[1:]
    else:
        peak_out, total_out, summed_out = refs[:3]
        refs = refs[3:]
    score_ref, weights_ref, values_ref, top_ref, total_ref, summed_ref = refs
    shard = lax.axis_index("ctx")
    pair = lax.axis_index("pair")
    rows, width = query_ref.shape
    half_rows = rows // heads // 2
    factor = LOG2E * width**-0.5
    starts = [jnp.int32(0)]
    for r in range(lengths_ref.shape[0] - 1):
        starts.append(starts[-1] + lengths_ref[r])

    def begin_of(position):
        begin = jnp.zeros_like(position)
        for start in starts[1:]:
            begin = jnp.where(start <= position, start, begin)
        return begin

    spans = []
    for shift, (cross, stay) in zip(sources, pieces):
        lead = order_ref[lax.rem(shard + shift, span_total // 2)]
        spans.append((lead, cross, stay, 0))
        spans.append((span_total - 1 - lead, cross, stay, 1))
    part_keys = pieces[0][0].shape[1] // 2
    keys_each = 2 * part_keys
    for number, (_, cross, stay, half) in enumerate(spans):
        for which, piece in enumerate((cross, stay)):
            values_ref[number, pl.ds(which * part_keys, part_keys), :] = piece[
                1, pl.ds(half * part_keys, part_keys), :
            ]
    lane = lax.broadcasted_iota(jnp.int32, (1, keys_each), 1)
    in_part = lax.rem(lane, part_keys)
    local = (
        in_part
        + jnp.where(in_part >= HALF_TOKENS, BLK - HALF_TOKENS, 0)
        + HALF_TOKENS * jnp.where(lane < part_keys, 1 - pair, pair)
    )

    tile_tokens = Q_TILE // heads
    tiles_half = half_rows // tile_tokens

    def tile(index, _):
        at = pl.ds(pl.multiple_of(index * Q_TILE, Q_TILE), Q_TILE)
        own_lead = order_ref[shard]
        query_span = jnp.where(index < tiles_half, own_lead, span_total - 1 - own_lead)
        first_pos = query_span * half_rows + lax.rem(index, tiles_half) * tile_tokens
        begin_low = begin_of(first_pos)
        near = []
        for span, _, _, _ in spans:
            near.append(
                (span * half_rows <= first_pos + tile_tokens - 1)
                & (span * half_rows + half_rows - 1 >= begin_low)
            )
        if first:
            top_ref[...] = jnp.full(top_ref.shape, FLOOR, jnp.float32)
        else:
            top_ref[...] = peak_in[at, :]

        for number, (span, cross, stay, half) in enumerate(spans):

            @pl.when(near[number])
            def _():
                part = pl.ds(half * part_keys, part_keys)
                score_ref[number] = lax.dot_general(
                    query_ref[at, :],
                    jnp.concatenate([cross[0, part, :], stay[0, part, :]], axis=0),
                    (((1,), (1,)), ((), ())),
                    preferred_element_type=jnp.float32,
                )
                key_pos = span * half_rows + local
                for row in range(0, Q_TILE, STRIP):
                    strip = pl.ds(row, STRIP)
                    index_in = lax.broadcasted_iota(jnp.int32, (STRIP, width), 0)
                    query_pos = first_pos + row // heads + index_in // heads
                    query_begin = begin_of(query_pos)
                    top = top_ref[strip, :]
                    for column in range(0, keys_each, width):
                        at_key = key_pos[:, column : column + width]
                        visible = (at_key <= query_pos) & (at_key >= query_begin)
                        score = score_ref[number, strip, column : column + width]
                        score = jnp.where(visible, score, MASKED)
                        score_ref[number, strip, column : column + width] = score
                        top = jnp.maximum(top, score)
                    top_ref[strip, :] = top

        for row in range(0, Q_TILE, STRIP):
            strip = pl.ds(row, STRIP)
            peak = jnp.max(top_ref[strip, :], axis=1, keepdims=True)
            peak = jnp.broadcast_to(peak, (STRIP, width))
            top_ref[strip, :] = peak
            rows_at = pl.ds(pl.multiple_of(index * Q_TILE + row, STRIP), STRIP)
            if first:
                total_ref[strip, :] = jnp.zeros((STRIP, width), jnp.float32)
                summed_ref[strip, :] = jnp.zeros((STRIP, width), jnp.float32)
            else:
                fade = jnp.exp2((peak_in[rows_at, :] - peak) * factor)
                total_ref[strip, :] = total_in[rows_at, :] * fade
                summed_ref[strip, :] = summed_in[rows_at, :] * fade
            if not last:
                peak_out[rows_at, :] = peak
        for number in range(len(spans)):

            @pl.when(near[number])
            def _():
                for row in range(0, Q_TILE, STRIP):
                    strip = pl.ds(row, STRIP)
                    peak = top_ref[strip, :]
                    total = total_ref[strip, :]
                    for column in range(0, keys_each, width):
                        score = score_ref[number, strip, column : column + width]
                        weight = jnp.exp2((score - peak) * factor)
                        total = total + weight
                        weights_ref[strip, column : column + width] = weight.astype(jnp.bfloat16)
                    total_ref[strip, :] = total
                summed_ref[...] += jnp.dot(
                    weights_ref[...], values_ref[number], preferred_element_type=jnp.float32
                )

        if last:
            total = jnp.sum(total_ref[...], axis=1, keepdims=True)
            out_ref[at, :] = (summed_ref[...] / total).astype(jnp.bfloat16)
        else:
            total_out[at, :] = total_ref[...]
            summed_out[at, :] = summed_ref[...]
        return 0

    lax.fori_loop(0, rows // Q_TILE, tile, 0)


def attend(order, lengths, query, pieces, sources, state, last, heads):
    rows, width = query.shape
    first = state is None
    smem = pl.BlockSpec(memory_space=pltpu.SMEM)
    vmem = pl.BlockSpec(memory_space=pltpu.VMEM)
    state = () if first else state
    if last:
        out_shape = jax.ShapeDtypeStruct((rows, width), jnp.bfloat16)
        out_specs = vmem
    else:
        out_shape = (jax.ShapeDtypeStruct((rows, width), jnp.float32),) * 3
        out_specs = (vmem,) * 3
    keys_each = pieces[0].shape[-2]
    count = 2 * len(sources)
    tile = pltpu.VMEM((Q_TILE, width), jnp.float32)
    return pl.pallas_call(
        functools.partial(attend_kernel, sources, first, last, 2 * order.shape[0], heads),
        out_shape=out_shape,
        in_specs=[smem, smem] + [vmem] * (1 + len(pieces) + len(state)),
        out_specs=out_specs,
        scratch_shapes=[
            pltpu.VMEM((count, Q_TILE, keys_each), jnp.float32),
            pltpu.VMEM((Q_TILE, keys_each), jnp.bfloat16),
            pltpu.VMEM((count, keys_each, width), jnp.bfloat16),
            tile,
            tile,
            tile,
        ],
        cost_estimate=pl.CostEstimate(
            flops=COST_FLOPS, bytes_accessed=4 * rows * width, transcendentals=0
        ),
        compiler_params=pltpu.CompilerParams(vmem_limit_bytes=24 * 2**20),
        name="attend",
    )(order, lengths, query, *pieces, *state)


def locate_slots(order_ref, partner_ref, found, shard, shard_count):
    for slot in range(CAP):
        found[0, slot] = -1
    for index in range(shard_count):
        lead = order_ref[index]
        shift = lax.rem(index - shard + shard_count, shard_count)
        found[1, lead] = shift
        found[2, lead] = 0
        found[1, 2 * shard_count - 1 - lead] = shift
        found[2, 2 * shard_count - 1 - lead] = 1
    taken = jnp.int32(0)
    for block in range(partner_ref.shape[0]):
        mine = partner_ref[block] == shard

        @pl.when(mine)
        def _():
            found[0, taken] = block

        taken = taken + mine.astype(jnp.int32)


def slot_place(found, slot):
    block = found[0, slot]
    span = jnp.maximum(block, 0) // 2
    place = found[2, span] * 2 + lax.rem(jnp.maximum(block, 0), 2)
    return block >= 0, found[1, span], place * HALF_TOKENS


def gather_pieces(pieces, count, held):
    for index, piece in enumerate(pieces):
        held[index // count, index % count] = piece[...]


def pick_kernel(found, *refs):
    out_ref, held = refs[-2:]
    count = held.shape[1]
    core = lax.axis_index("tp")
    share = HALF_TOKENS // 2
    gather_pieces(refs[: 2 * count], count, held)
    for slot in range(CAP):
        live, index, start = slot_place(found, slot)
        begin = pl.ds(pl.multiple_of(start + (1 - core) * share, share), share)
        for which in range(2):
            for kind in range(2):
                out_ref[slot, kind, which] = held[which, index, kind, begin, :]


def slot_call(kernel, out_shape, scratch, name, count, operands, piece_shape):
    smem = pl.BlockSpec(memory_space=pltpu.SMEM)
    vmem = pl.BlockSpec(memory_space=pltpu.VMEM)
    return pl.pallas_call(
        kernel,
        out_shape=out_shape,
        in_specs=[smem] + [vmem] * (len(operands) - 1),
        out_specs=vmem,
        scratch_shapes=[pltpu.VMEM((2, count) + piece_shape, jnp.bfloat16)] + scratch,
        compiler_params=pltpu.CompilerParams(vmem_limit_bytes=12 * 2**20),
        name=name,
    )(*operands)


def pick(found, stay, cross):
    piece_shape = cross[0].shape
    out_shape = jax.ShapeDtypeStruct((CAP, 2, 2, HALF_TOKENS // 2, piece_shape[2]), jnp.bfloat16)
    operands = (found, *stay, *cross)
    return slot_call(pick_kernel, out_shape, [], "pick_slots", len(stay), operands, piece_shape)


def place_kernel(found, *refs):
    given_ref, out_ref, held, wide = refs[-4:]
    count = held.shape[1]
    pair = lax.axis_index("pair")
    core = lax.axis_index("tp")
    share = HALF_TOKENS // 2
    gather_pieces(refs[: 2 * count], count, held)
    for slot in range(CAP):
        live, index, start = slot_place(found, slot)
        begin = pl.ds(pl.multiple_of(start + core * share, share), share)
        for which in range(2):
            group = 2 * (pair if which == 0 else 1 - pair)
            for kind in range(2):
                base = (slot * 2 + kind) * share * 4 + group
                kept = held[which, index, kind, begin, :].astype(jnp.float32)
                given = given_ref[slot, kind, which].astype(jnp.float32)
                wide[pl.ds(base + core, share, stride=4), :] = jnp.where(live, kept, 0.0)
                wide[pl.ds(base + 1 - core, share, stride=4), :] = jnp.where(live, given, 0.0)
    out_ref[...] = wide[...].astype(jnp.bfloat16)


def place(found, stay, cross, given):
    piece_shape = cross[0].shape
    rows = CAP * 2 * (HALF_TOKENS // 2) * 4
    out_shape = jax.ShapeDtypeStruct((rows, piece_shape[2]), jnp.bfloat16)
    scratch = [pltpu.VMEM((rows, piece_shape[2]), jnp.float32)]
    operands = (found, *stay, *cross, given)
    return slot_call(place_kernel, out_shape, scratch, "place_slots", len(stay), operands, piece_shape)


def ring(array, step, count):
    return lax.ppermute(array, "ctx", [(i, (i + step) % count) for i in range(count)])


def swap(array, axis):
    return lax.ppermute(array, axis, [(0, 1), (1, 0)])


def after(value, earlier):
    return lax.optimization_barrier((value, earlier))


def pieces_program(queries, keys, values, span_order, lengths, kv_partner):
    count = lax.axis_size("ctx")
    query_rows, heads, width = queries.shape
    partner = kv_partner[:, 0]
    query = queries.reshape(query_rows * heads, width)
    keys_flat = keys.reshape(-1, width)
    values_flat = values.reshape(-1, width)
    keys_other = swap(keys, "tp").reshape(-1, width)
    values_other = swap(values, "tp").reshape(-1, width)
    own = jnp.stack([keys_flat, values_flat]).astype(jnp.float32)
    cross0 = split_heads(own, keys_other, values_other, True)
    keys_other, _ = after(keys_other, cross0)
    stay0 = split_heads(own, keys_other, values_other, False)
    partner, _ = after(partner, stay0)
    found = find(span_order, partner)

    def step(pieces, sources, state, last=False):
        return attend(span_order, lengths, query, pieces, sources, state, last, heads)

    cross3 = ring(cross0, 1, count)
    cross1 = ring(cross0, -1, count)
    stay3 = ring(stay0, 1, count)
    stay1 = ring(stay0, -1, count)
    over0 = swap(cross0, "pair")
    state = step((cross0, stay0), (0,), None)
    cross2 = ring(cross3, 1, count)
    over3 = swap(cross3, "pair")
    over1 = swap(cross1, "pair")
    stay2 = ring(stay3, 1, count)
    state = step((cross3, stay3, cross1, stay1), (3, 1), state)
    over2 = swap(cross2, "pair")
    stay = (stay0, stay1, stay2, stay3)
    over = (over0, over1, over2, over3)
    picked = pick(found, stay, over)
    given = swap(picked, "tp")
    cross2, _ = after(cross2, picked)
    attended = step((cross2, stay2), (2,), state, True)
    cache = place(found, stay, over, given)
    return attended.reshape(queries.shape), cache.reshape(CAP, 2, HALF_TOKENS // 2, 4, width)


def pick_program(mesh):
    sizes = mesh.shape
    fits = sizes["ctx"] == 4 and sizes["pair"] == 2 and sizes["tp"] == 2
    return pieces_program if fits else shards


def solution(mesh):
    return jax.shard_map(
        pick_program(mesh),
        mesh=mesh,
        in_specs=(
            P(("groups", "ctx"), ("pair", "tp"), None),
            P(("groups", "ctx", "tp"), "pair", None),
            P(("groups", "ctx", "tp"), "pair", None),
            P("groups"),
            P("groups"),
            P("groups", None),
        ),
        out_specs=(
            P(("groups", "ctx"), ("pair", "tp"), None),
            P(("groups", "ctx"), None, ("pair", "tp"), None, None),
        ),
        check_vma=False,
    )
```

```python
import functools

import jax
import jax.numpy as jnp
from jax import lax
from jax.experimental import pallas as pl
from jax.experimental.pallas import tpu as pltpu
from jax.sharding import PartitionSpec as P

GROUP = 4
BLK = 128
CAP = 8


neg_big = -1e30
key_block = 1024


def lookup(entries, where_at):
    entry_count = entries.shape[0]
    matches = where_at[..., None] == jnp.arange(entry_count, dtype=jnp.int32)
    return jnp.sum(jnp.where(matches, entries, 0), axis=-1)


def row_position(row_index, span_order, span_total, half_rows):
    block_index = row_index // half_rows
    leading = lookup(span_order, block_index // 2)
    span_index = jnp.where(block_index % 2 == 0, leading, span_total - 1 - leading)
    return span_index * half_rows + row_index % half_rows


def position_row(position, span_order, span_total, half_rows):
    span_index = position // half_rows
    shard_index = jnp.arange(span_order.shape[0], dtype=jnp.int32)
    even_match = span_order == span_index[..., None]
    odd_match = span_total - 1 - span_order == span_index[..., None]
    block_index = jnp.sum(
        jnp.where(even_match, 2 * shard_index, 0) + jnp.where(odd_match, 2 * shard_index + 1, 0),
        axis=-1,
    )
    return block_index * half_rows + position % half_rows


def request_of(position, lengths):
    boundary = jnp.cumsum(lengths)
    return jnp.sum((boundary <= position[..., None]).astype(jnp.int32), axis=-1)


def keep_state(inner):
    return inner


def shards(queries, keys, values, span_order, lengths, kv_partner):
    pair_count = lax.axis_size("pair")
    core_count = lax.axis_size("tp")
    span_total = 2 * lax.axis_size("ctx")
    ctx_index = lax.axis_index("ctx")
    core_index = lax.axis_index("tp")
    query_rows, local_heads, head_width = queries.shape
    half_rows = query_rows // 2
    local_groups = keys.shape[1]
    scale = head_width ** (-0.5)
    query_pos = row_position(
        ctx_index * query_rows + jnp.arange(query_rows, dtype=jnp.int32),
        span_order,
        span_total,
        half_rows,
    )
    query_req = request_of(query_pos, lengths)
    partner = kv_partner[:, 0]
    block_index = jnp.arange(partner.shape[0], dtype=jnp.int32)
    earlier = (partner[None, :] == partner[:, None]) & (block_index[None, :] < block_index[:, None])
    rank = jnp.sum(earlier.astype(jnp.int32), axis=1)
    slot_index = jnp.arange(CAP, dtype=jnp.int32)
    taken = (partner[None, :] == ctx_index) & (rank[None, :] == slot_index[:, None])
    slot_live = jnp.any(taken, axis=1)
    slot_block = jnp.sum(jnp.where(taken, block_index[None, :], 0), axis=1)
    token_share = BLK // (pair_count * core_count)
    pair_index = jnp.arange(pair_count, dtype=jnp.int32)

    def make_absorb(query_block, kv_pick, gathered_row, target, live):

        def attend(state, block_keys, block_values, key_rows):
            key_pos = row_position(key_rows, span_order, span_total, half_rows)
            key_req = request_of(key_pos, lengths)
            visible = (key_pos[None, :] <= query_pos[:, None]) & (
                key_req[None, :] == query_req[:, None]
            )

            def update(inner):
                peak, total, summed = inner
                head_keys = jnp.take(block_keys, kv_pick, axis=1)
                head_values = jnp.take(block_values, kv_pick, axis=1)
                scores = (
                    jnp.einsum(
                        "rhd,nhd->rhn", query_block, head_keys, preferred_element_type=jnp.float32
                    )
                    * scale
                )
                scores = jnp.where(visible[:, None, :], scores, neg_big)
                new_peak = jnp.maximum(peak, jnp.max(scores, axis=2))
                weights = jnp.where(
                    visible[:, None, :], jnp.exp(scores - new_peak[:, :, None]), 0.0
                )
                factor = jnp.exp(peak - new_peak)
                new_total = total * factor + jnp.sum(weights, axis=2)
                product = jnp.einsum(
                    "rhn,nhd->rhd",
                    weights.astype(jnp.bfloat16),
                    head_values,
                    preferred_element_type=jnp.float32,
                )
                return (new_peak, new_total, summed * factor[:, :, None] + product)

            return lax.cond(jnp.any(visible), update, keep_state, state)

        def absorb(carry, piece, start):
            state, selected = carry
            piece_keys, piece_values = piece
            count = piece_keys.shape[0]
            inside = live & (target >= 0) & (target < count)
            safe = jnp.clip(target, 0, count - 1)
            picked = jnp.stack(
                [jnp.take(piece_keys, safe, axis=0), jnp.take(piece_values, safe, axis=0)], axis=1
            )
            selected = jnp.where(
                inside[:, None, :, :, :, None, None], picked, jnp.zeros((), jnp.bfloat16)
            )
            turns = count // key_block
            shaped_keys = piece_keys.reshape(turns, key_block, local_groups, head_width)
            shaped_values = piece_values.reshape(turns, key_block, local_groups, head_width)
            block_starts = key_block * jnp.arange(turns, dtype=jnp.int32)

            def one_block(inner, items):
                block_keys, block_values, block_start = items
                key_rows = gathered_row(block_start + jnp.arange(key_block, dtype=jnp.int32))
                return (attend(inner, block_keys, block_values, key_rows), None)

            state, _ = lax.scan(one_block, state, (shaped_keys, shaped_values, block_starts))
            return (state, selected)

        return absorb

    def same_rows(row_index):
        return row_index

    kv_pick = (core_index * local_heads + jnp.arange(local_heads, dtype=jnp.int32)) // GROUP
    ranges = pair_index[:, None] * core_count + jnp.reshape(core_index, (1,))[None, :]
    wanted = (
        slot_block[:, None, None, None] * BLK
        + ranges[None, :, :, None] * token_share
        + jnp.arange(token_share, dtype=jnp.int32)[None, None, None, :]
    )
    target = position_row(wanted, span_order, span_total, half_rows)
    live = jnp.broadcast_to(slot_live[:, None, None, None], target.shape)
    absorb = make_absorb(queries, kv_pick, same_rows, target, live)
    state = (
        jnp.full((query_rows, local_heads), neg_big, jnp.float32),
        jnp.zeros((query_rows, local_heads), jnp.float32),
        jnp.zeros((query_rows, local_heads, head_width), jnp.float32),
    )
    selected = jnp.zeros(
        target.shape[:1] + (2,) + target.shape[1:] + (local_groups, head_width), jnp.bfloat16
    )
    (peak, total, summed), selected = absorb(
        (state, selected),
        (
            lax.all_gather(keys, ("ctx", "tp"), axis=0, tiled=True),
            lax.all_gather(values, ("ctx", "tp"), axis=0, tiled=True),
        ),
        jnp.int32(0),
    )
    selected = selected[:, :, :, 0]
    attended = (summed / total[:, :, None]).astype(jnp.bfloat16)
    received = lax.all_to_all(selected, "pair", split_axis=2, concat_axis=4, tiled=True)
    decode_cache = received.reshape(CAP, 2, token_share, pair_count * local_groups, head_width)
    return (attended, decode_cache)


HALF_TOKENS = BLK // 2
LOG2E = 1.4426950408889634
MASKED = -1e30
FLOOR = -1e29
COST_FLOPS = 4 * 10**9
Q_TILE = 1024
STRIP = 512


def split_kernel(cross, own_ref, key_other, value_other, out_ref, wide):
    pair = lax.axis_index("pair")
    core = lax.axis_index("tp")
    part = 1 - pair if cross else pair
    for kind, other in enumerate((key_other, value_other)):
        wide[kind, core] = own_ref[kind]
        wide[kind, 1 - core] = other[...].astype(jnp.float32)
    for kind in range(2):
        for block in range(4):
            first = (block % 2) * 2 * BLK + part * 2 * HALF_TOKENS + core
            rows = wide[kind, block // 2, pl.ds(first, HALF_TOKENS, stride=2), :]
            out_ref[kind, pl.ds(block * HALF_TOKENS, HALF_TOKENS), :] = rows.astype(jnp.bfloat16)


def split_heads(own, keys_other, values_other, cross):
    _, rows, width = own.shape
    return pl.pallas_call(
        functools.partial(split_kernel, cross),
        out_shape=jax.ShapeDtypeStruct((2, rows // 2, width), jnp.bfloat16),
        scratch_shapes=[pltpu.VMEM((2, 2, rows, width), jnp.float32)],
        compiler_params=pltpu.CompilerParams(vmem_limit_bytes=12 * 2**20),
        name="split_heads",
    )(own, keys_other, values_other)


def attend_kernel(sources, first, last, span_total, heads, *refs):
    order_ref, lengths_ref, _, query_ref = refs[:4]
    refs = refs[4:]
    pieces = []
    for _ in sources:
        pieces.append((refs[0], refs[1]))
        refs = refs[2:]
    if not first:
        peak_in, total_in, summed_in = refs[:3]
        refs = refs[3:]
    if last:
        out_ref, refs = refs[0], refs[1:]
    else:
        peak_out, total_out, summed_out = refs[:3]
        refs = refs[3:]
    values_ref, top_ref, total_ref, summed_ref = refs
    shard = lax.axis_index("ctx")
    pair = lax.axis_index("pair")
    rows, width = query_ref.shape
    half_rows = rows // heads // 2
    factor = LOG2E * width**-0.5
    starts = [jnp.int32(0)]
    for r in range(lengths_ref.shape[0] - 1):
        starts.append(starts[-1] + lengths_ref[r])

    def begin_of(position):
        begin = jnp.zeros_like(position)
        for start in starts[1:]:
            begin = jnp.where(start <= position, start, begin)
        return begin

    spans = []
    for shift, (cross, stay) in zip(sources, pieces):
        lead = order_ref[lax.rem(shard + shift, span_total // 2)]
        spans.append((lead, cross, stay, 0))
        spans.append((span_total - 1 - lead, cross, stay, 1))
    part_keys = pieces[0][0].shape[1] // 2
    keys_each = 2 * part_keys
    for number, (_, cross, stay, half) in enumerate(spans):
        for which, piece in enumerate((cross, stay)):
            values_ref[number, pl.ds(which * part_keys, part_keys), :] = piece[
                1, pl.ds(half * part_keys, part_keys), :
            ]
    lane = lax.broadcasted_iota(jnp.int32, (1, keys_each), 1)
    in_part = lax.rem(lane, part_keys)
    local = (
        in_part
        + jnp.where(in_part >= HALF_TOKENS, BLK - HALF_TOKENS, 0)
        + HALF_TOKENS * jnp.where(lane < part_keys, 1 - pair, pair)
    )

    tile_tokens = Q_TILE // heads
    tiles_half = half_rows // tile_tokens

    def tile(index, _):
        at = pl.ds(pl.multiple_of(index * Q_TILE, Q_TILE), Q_TILE)
        own_lead = order_ref[shard]
        query_span = jnp.where(index < tiles_half, own_lead, span_total - 1 - own_lead)
        first_pos = query_span * half_rows + lax.rem(index, tiles_half) * tile_tokens
        begin_low = begin_of(first_pos)
        near = []
        for span, _, _, _ in spans:
            near.append(
                (span * half_rows <= first_pos + tile_tokens - 1)
                & (span * half_rows + half_rows - 1 >= begin_low)
            )
        if first:
            top_ref[...] = jnp.full(top_ref.shape, FLOOR, jnp.float32)
            total_ref[...] = jnp.zeros(total_ref.shape, jnp.float32)
            summed_ref[...] = jnp.zeros(summed_ref.shape, jnp.float32)
        else:
            top_ref[...] = peak_in[at, :]
            total_ref[...] = total_in[at, :]
            summed_ref[...] = summed_in[at, :]

        for number, (span, cross, stay, half) in enumerate(spans):

            @pl.when(near[number])
            def _():
                part = pl.ds(half * part_keys, part_keys)
                keys = jnp.concatenate([cross[0, part, :], stay[0, part, :]], axis=0)
                key_pos = span * half_rows + local
                index_in = lax.broadcasted_iota(jnp.int32, (STRIP, width), 0) // heads
                for row in range(0, Q_TILE, STRIP):
                    strip = pl.ds(row, STRIP)
                    rows_at = pl.ds(pl.multiple_of(index * Q_TILE + row, STRIP), STRIP)
                    score = lax.dot_general(
                        query_ref[rows_at, :],
                        keys,
                        (((1,), (1,)), ((), ())),
                        preferred_element_type=jnp.float32,
                    )
                    query_pos = first_pos + row // heads + index_in
                    query_begin = begin_of(query_pos)
                    old = top_ref[strip, :]
                    top = old
                    masked = []
                    for column in range(0, keys_each, width):
                        at_key = key_pos[:, column : column + width]
                        visible = (at_key <= query_pos) & (at_key >= query_begin)
                        masked.append(
                            jnp.where(visible, score[:, column : column + width], MASKED)
                        )
                        top = jnp.maximum(top, masked[-1])
                    peak = jnp.broadcast_to(
                        jnp.max(top, axis=1, keepdims=True), (STRIP, width)
                    )
                    top_ref[strip, :] = peak
                    fade = jnp.exp2((old - peak) * factor)
                    total = total_ref[strip, :] * fade
                    weights = []
                    for part_score in masked:
                        weight = jnp.exp2((part_score - peak) * factor)
                        total = total + weight
                        weights.append(weight.astype(jnp.bfloat16))
                    total_ref[strip, :] = total
                    summed_ref[strip, :] = summed_ref[strip, :] * fade + jnp.dot(
                        jnp.concatenate(weights, axis=1),
                        values_ref[number],
                        preferred_element_type=jnp.float32,
                    )

        if not last:
            peak_out[at, :] = top_ref[...]
        if last:
            total = jnp.sum(total_ref[...], axis=1, keepdims=True)
            out_ref[at, :] = (summed_ref[...] / total).astype(jnp.bfloat16)
        else:
            total_out[at, :] = total_ref[...]
            summed_out[at, :] = summed_ref[...]
        return 0

    lax.fori_loop(0, rows // Q_TILE, tile, 0)


def attend(order, lengths, partner, query, pieces, sources, state, last, heads):
    rows, width = query.shape
    first = state is None
    smem = pl.BlockSpec(memory_space=pltpu.SMEM)
    vmem = pl.BlockSpec(memory_space=pltpu.VMEM)
    state = () if first else state
    if last:
        out_shape = jax.ShapeDtypeStruct((rows, width), jnp.bfloat16)
        out_specs = vmem
    else:
        out_shape = (jax.ShapeDtypeStruct((rows, width), jnp.float32),) * 3
        out_specs = (vmem,) * 3
    keys_each = pieces[0].shape[-2]
    count = 2 * len(sources)
    tile = pltpu.VMEM((Q_TILE, width), jnp.float32)
    return pl.pallas_call(
        functools.partial(attend_kernel, sources, first, last, 2 * order.shape[0], heads),
        out_shape=out_shape,
        in_specs=[smem] * 3 + [vmem] * (1 + len(pieces) + len(state)),
        out_specs=out_specs,
        scratch_shapes=[
            pltpu.VMEM((count, keys_each, width), jnp.bfloat16),
            tile,
            tile,
            tile,
        ],
        cost_estimate=pl.CostEstimate(
            flops=COST_FLOPS, bytes_accessed=4 * rows * width, transcendentals=0
        ),
        compiler_params=pltpu.CompilerParams(vmem_limit_bytes=24 * 2**20),
        name="attend",
    )(order, lengths, partner, query, *pieces, *state)


def locate_slots(order_ref, partner_ref, found, shard, shard_count):
    for slot in range(CAP):
        found[0, slot] = -1
    for index in range(shard_count):
        lead = order_ref[index]
        shift = lax.rem(index - shard + shard_count, shard_count)
        found[1, lead] = shift
        found[2, lead] = 0
        found[1, 2 * shard_count - 1 - lead] = shift
        found[2, 2 * shard_count - 1 - lead] = 1
    taken = jnp.int32(0)
    for block in range(partner_ref.shape[0]):
        mine = partner_ref[block] == shard

        @pl.when(mine)
        def _():
            found[0, taken] = block

        taken = taken + mine.astype(jnp.int32)


def slot_place(found, slot):
    block = found[0, slot]
    span = jnp.maximum(block, 0) // 2
    place = found[2, span] * 2 + lax.rem(jnp.maximum(block, 0), 2)
    return block >= 0, found[1, span], place * HALF_TOKENS


def gather_pieces(pieces, count, held):
    for index, piece in enumerate(pieces):
        held[index // count, index % count] = piece[...]


def pick_kernel(order_ref, partner_ref, *refs):
    given_ref, kept_ref, held, found = refs[-4:]
    count = held.shape[1]
    core = lax.axis_index("tp")
    share = HALF_TOKENS // 2
    gather_pieces(refs[: 2 * count], count, held)
    locate_slots(order_ref, partner_ref, found, lax.axis_index("ctx"), count)
    for slot in range(CAP):
        live, index, start = slot_place(found, slot)
        for out_ref, half in ((given_ref, 1 - core), (kept_ref, core)):
            begin = pl.ds(pl.multiple_of(start + half * share, share), share)
            for which in range(2):
                for kind in range(2):
                    rows = held[which, index, kind, begin, :]
                    out_ref[slot, kind, which] = jnp.where(live, rows, jnp.zeros_like(rows))


def pick(order, partner, stay, cross):
    smem = pl.BlockSpec(memory_space=pltpu.SMEM)
    vmem = pl.BlockSpec(memory_space=pltpu.VMEM)
    count = len(stay)
    piece_shape = cross[0].shape
    rows = jax.ShapeDtypeStruct((CAP, 2, 2, HALF_TOKENS // 2, piece_shape[2]), jnp.bfloat16)
    return pl.pallas_call(
        pick_kernel,
        out_shape=(rows, rows),
        in_specs=[smem, smem] + [vmem] * (2 * count),
        out_specs=(vmem, vmem),
        scratch_shapes=[
            pltpu.VMEM((2, count) + piece_shape, jnp.bfloat16),
            pltpu.SMEM((3, max(CAP, 2 * count)), jnp.int32),
        ],
        compiler_params=pltpu.CompilerParams(vmem_limit_bytes=12 * 2**20),
        name="pick_slots",
    )(order, partner, *stay, *cross)


def place_kernel(kept_ref, given_ref, out_ref, wide):
    pair = lax.axis_index("pair")
    core = lax.axis_index("tp")
    share = kept_ref.shape[3]
    for slot in range(CAP):
        for kind in range(2):
            for which in range(2):
                base = (slot * 2 + kind) * share * 4 + 2 * (pair if which == 0 else 1 - pair)
                for ref, head in ((kept_ref, core), (given_ref, 1 - core)):
                    rows = ref[slot, kind, which].astype(jnp.float32)
                    wide[pl.ds(base + head, share, stride=4), :] = rows
    out_ref[...] = wide[...].astype(jnp.bfloat16)


def place(kept, given):
    rows, width = CAP * 2 * kept.shape[3] * 4, kept.shape[4]
    return pl.pallas_call(
        place_kernel,
        out_shape=jax.ShapeDtypeStruct((rows, width), jnp.bfloat16),
        scratch_shapes=[pltpu.VMEM((rows, width), jnp.float32)],
        compiler_params=pltpu.CompilerParams(vmem_limit_bytes=12 * 2**20),
        name="place_slots",
    )(kept, given)


def ring(array, step, count):
    return lax.ppermute(array, "ctx", [(i, (i + step) % count) for i in range(count)])


def swap(array, axis):
    return lax.ppermute(array, axis, [(0, 1), (1, 0)])


def after(value, earlier):
    return lax.optimization_barrier((value, earlier))


def pieces_program(queries, keys, values, span_order, lengths, kv_partner):
    count = lax.axis_size("ctx")
    query_rows, heads, width = queries.shape
    partner = kv_partner[:, 0]
    query = queries.reshape(query_rows * heads, width)
    keys_flat = keys.reshape(-1, width)
    values_flat = values.reshape(-1, width)
    keys_other = swap(keys, "tp").reshape(-1, width)
    values_other = swap(values, "tp").reshape(-1, width)
    own = jnp.stack([keys_flat, values_flat]).astype(jnp.float32)
    cross0 = split_heads(own, keys_other, values_other, True)
    keys_other, _ = after(keys_other, cross0)
    stay0 = split_heads(own, keys_other, values_other, False)

    def step(pieces, sources, state, last=False):
        return attend(span_order, lengths, partner, query, pieces, sources, state, last, heads)

    cross3 = ring(cross0, 1, count)
    cross1 = ring(cross0, -1, count)
    stay3 = ring(stay0, 1, count)
    stay1 = ring(stay0, -1, count)
    over0 = swap(cross0, "pair")
    state = step((cross0, stay0), (0,), None)
    cross2 = ring(cross3, 1, count)
    over3 = swap(cross3, "pair")
    over1 = swap(cross1, "pair")
    stay2 = ring(stay3, 1, count)
    state = step((cross3, stay3, cross1, stay1), (3, 1), state)
    over2 = swap(cross2, "pair")
    stay = (stay0, stay1, stay2, stay3)
    over = (over0, over1, over2, over3)
    picked, kept = pick(span_order, partner, stay, over)
    given = swap(picked, "tp")
    cross2, _ = after(cross2, picked)
    attended = step((cross2, stay2), (2,), state, True)
    cache = place(kept, given)
    return attended.reshape(queries.shape), cache.reshape(CAP, 2, HALF_TOKENS // 2, 4, width)


def pick_program(mesh):
    sizes = mesh.shape
    fits = sizes["ctx"] == 4 and sizes["pair"] == 2 and sizes["tp"] == 2
    return pieces_program if fits else shards


def solution(mesh):
    return jax.shard_map(
        pick_program(mesh),
        mesh=mesh,
        in_specs=(
            P(("groups", "ctx"), ("pair", "tp"), None),
            P(("groups", "ctx", "tp"), "pair", None),
            P(("groups", "ctx", "tp"), "pair", None),
            P("groups"),
            P("groups"),
            P("groups", None),
        ),
        out_specs=(
            P(("groups", "ctx"), ("pair", "tp"), None),
            P(("groups", "ctx"), None, ("pair", "tp"), None, None),
        ),
        check_vma=False,
    )
```

```python
import functools

import jax
import jax.numpy as jnp
from jax import lax
from jax.experimental import pallas as pl
from jax.experimental.pallas import tpu as pltpu
from jax.sharding import PartitionSpec as P

GROUP = 4
BLK = 128
CAP = 8


neg_big = -1e30
key_block = 1024


def lookup(entries, where_at):
    entry_count = entries.shape[0]
    matches = where_at[..., None] == jnp.arange(entry_count, dtype=jnp.int32)
    return jnp.sum(jnp.where(matches, entries, 0), axis=-1)


def row_position(row_index, span_order, span_total, half_rows):
    block_index = row_index // half_rows
    leading = lookup(span_order, block_index // 2)
    span_index = jnp.where(block_index % 2 == 0, leading, span_total - 1 - leading)
    return span_index * half_rows + row_index % half_rows


def position_row(position, span_order, span_total, half_rows):
    span_index = position // half_rows
    shard_index = jnp.arange(span_order.shape[0], dtype=jnp.int32)
    even_match = span_order == span_index[..., None]
    odd_match = span_total - 1 - span_order == span_index[..., None]
    block_index = jnp.sum(
        jnp.where(even_match, 2 * shard_index, 0) + jnp.where(odd_match, 2 * shard_index + 1, 0),
        axis=-1,
    )
    return block_index * half_rows + position % half_rows


def request_of(position, lengths):
    boundary = jnp.cumsum(lengths)
    return jnp.sum((boundary <= position[..., None]).astype(jnp.int32), axis=-1)


def keep_state(inner):
    return inner


def shards(queries, keys, values, span_order, lengths, kv_partner):
    pair_count = lax.axis_size("pair")
    core_count = lax.axis_size("tp")
    span_total = 2 * lax.axis_size("ctx")
    ctx_index = lax.axis_index("ctx")
    core_index = lax.axis_index("tp")
    query_rows, local_heads, head_width = queries.shape
    half_rows = query_rows // 2
    local_groups = keys.shape[1]
    scale = head_width ** (-0.5)
    query_pos = row_position(
        ctx_index * query_rows + jnp.arange(query_rows, dtype=jnp.int32),
        span_order,
        span_total,
        half_rows,
    )
    query_req = request_of(query_pos, lengths)
    partner = kv_partner[:, 0]
    block_index = jnp.arange(partner.shape[0], dtype=jnp.int32)
    earlier = (partner[None, :] == partner[:, None]) & (block_index[None, :] < block_index[:, None])
    rank = jnp.sum(earlier.astype(jnp.int32), axis=1)
    slot_index = jnp.arange(CAP, dtype=jnp.int32)
    taken = (partner[None, :] == ctx_index) & (rank[None, :] == slot_index[:, None])
    slot_live = jnp.any(taken, axis=1)
    slot_block = jnp.sum(jnp.where(taken, block_index[None, :], 0), axis=1)
    token_share = BLK // (pair_count * core_count)
    pair_index = jnp.arange(pair_count, dtype=jnp.int32)

    def make_absorb(query_block, kv_pick, gathered_row, target, live):

        def attend(state, block_keys, block_values, key_rows):
            key_pos = row_position(key_rows, span_order, span_total, half_rows)
            key_req = request_of(key_pos, lengths)
            visible = (key_pos[None, :] <= query_pos[:, None]) & (
                key_req[None, :] == query_req[:, None]
            )

            def update(inner):
                peak, total, summed = inner
                head_keys = jnp.take(block_keys, kv_pick, axis=1)
                head_values = jnp.take(block_values, kv_pick, axis=1)
                scores = (
                    jnp.einsum(
                        "rhd,nhd->rhn", query_block, head_keys, preferred_element_type=jnp.float32
                    )
                    * scale
                )
                scores = jnp.where(visible[:, None, :], scores, neg_big)
                new_peak = jnp.maximum(peak, jnp.max(scores, axis=2))
                weights = jnp.where(
                    visible[:, None, :], jnp.exp(scores - new_peak[:, :, None]), 0.0
                )
                factor = jnp.exp(peak - new_peak)
                new_total = total * factor + jnp.sum(weights, axis=2)
                product = jnp.einsum(
                    "rhn,nhd->rhd",
                    weights.astype(jnp.bfloat16),
                    head_values,
                    preferred_element_type=jnp.float32,
                )
                return (new_peak, new_total, summed * factor[:, :, None] + product)

            return lax.cond(jnp.any(visible), update, keep_state, state)

        def absorb(carry, piece, start):
            state, selected = carry
            piece_keys, piece_values = piece
            count = piece_keys.shape[0]
            inside = live & (target >= 0) & (target < count)
            safe = jnp.clip(target, 0, count - 1)
            picked = jnp.stack(
                [jnp.take(piece_keys, safe, axis=0), jnp.take(piece_values, safe, axis=0)], axis=1
            )
            selected = jnp.where(
                inside[:, None, :, :, :, None, None], picked, jnp.zeros((), jnp.bfloat16)
            )
            turns = count // key_block
            shaped_keys = piece_keys.reshape(turns, key_block, local_groups, head_width)
            shaped_values = piece_values.reshape(turns, key_block, local_groups, head_width)
            block_starts = key_block * jnp.arange(turns, dtype=jnp.int32)

            def one_block(inner, items):
                block_keys, block_values, block_start = items
                key_rows = gathered_row(block_start + jnp.arange(key_block, dtype=jnp.int32))
                return (attend(inner, block_keys, block_values, key_rows), None)

            state, _ = lax.scan(one_block, state, (shaped_keys, shaped_values, block_starts))
            return (state, selected)

        return absorb

    def same_rows(row_index):
        return row_index

    kv_pick = (core_index * local_heads + jnp.arange(local_heads, dtype=jnp.int32)) // GROUP
    ranges = pair_index[:, None] * core_count + jnp.reshape(core_index, (1,))[None, :]
    wanted = (
        slot_block[:, None, None, None] * BLK
        + ranges[None, :, :, None] * token_share
        + jnp.arange(token_share, dtype=jnp.int32)[None, None, None, :]
    )
    target = position_row(wanted, span_order, span_total, half_rows)
    live = jnp.broadcast_to(slot_live[:, None, None, None], target.shape)
    absorb = make_absorb(queries, kv_pick, same_rows, target, live)
    state = (
        jnp.full((query_rows, local_heads), neg_big, jnp.float32),
        jnp.zeros((query_rows, local_heads), jnp.float32),
        jnp.zeros((query_rows, local_heads, head_width), jnp.float32),
    )
    selected = jnp.zeros(
        target.shape[:1] + (2,) + target.shape[1:] + (local_groups, head_width), jnp.bfloat16
    )
    (peak, total, summed), selected = absorb(
        (state, selected),
        (
            lax.all_gather(keys, ("ctx", "tp"), axis=0, tiled=True),
            lax.all_gather(values, ("ctx", "tp"), axis=0, tiled=True),
        ),
        jnp.int32(0),
    )
    selected = selected[:, :, :, 0]
    attended = (summed / total[:, :, None]).astype(jnp.bfloat16)
    received = lax.all_to_all(selected, "pair", split_axis=2, concat_axis=4, tiled=True)
    decode_cache = received.reshape(CAP, 2, token_share, pair_count * local_groups, head_width)
    return (attended, decode_cache)


HALF_TOKENS = BLK // 2
LOG2E = 1.4426950408889634
MASKED = -1e30
FLOOR = -1e29
COST_FLOPS = 4 * 10**9
Q_TILE = 1024
STRIP = 512
PLACE_GROUPS = 4


def split_kernel(cross, own_ref, key_other, value_other, out_ref, wide):
    pair = lax.axis_index("pair")
    core = lax.axis_index("tp")
    part = 1 - pair if cross else pair
    for kind, other in enumerate((key_other, value_other)):
        wide[kind, core] = own_ref[kind]
        wide[kind, 1 - core] = other[...].astype(jnp.float32)
    for kind in range(2):
        for block in range(4):
            first = (block % 2) * 2 * BLK + part * 2 * HALF_TOKENS + core
            rows = wide[kind, block // 2, pl.ds(first, HALF_TOKENS, stride=2), :]
            out_ref[kind, pl.ds(block * HALF_TOKENS, HALF_TOKENS), :] = rows.astype(jnp.bfloat16)


def split_heads(own, keys_other, values_other, cross):
    _, rows, width = own.shape
    return pl.pallas_call(
        functools.partial(split_kernel, cross),
        out_shape=jax.ShapeDtypeStruct((2, rows // 2, width), jnp.bfloat16),
        scratch_shapes=[pltpu.VMEM((2, 2, rows, width), jnp.float32)],
        compiler_params=pltpu.CompilerParams(vmem_limit_bytes=12 * 2**20),
        name="split_heads",
    )(own, keys_other, values_other)


def attend_kernel(sources, first, last, span_total, heads, *refs):
    order_ref, lengths_ref, _, query_ref = refs[:4]
    refs = refs[4:]
    pieces = []
    for _, kinds in sources:
        pieces.append(refs[: len(kinds)])
        refs = refs[len(kinds) :]
    if not first:
        peak_in, total_in, summed_in = refs[:3]
        refs = refs[3:]
    if last:
        out_ref, refs = refs[0], refs[1:]
    else:
        peak_out, total_out, summed_out = refs[:3]
        refs = refs[3:]
    values_ref, top_ref, total_ref, summed_ref = refs[:4]
    if last:
        result_ref, sems = refs[4:]

    def send_strip(number):
        at = pl.ds(pl.multiple_of(number * STRIP, STRIP), STRIP)
        return pltpu.make_async_copy(result_ref.at[at, :], out_ref.at[at, :], sems.at[number])

    shard = lax.axis_index("ctx")
    pair = lax.axis_index("pair")
    rows, width = query_ref.shape
    half_rows = rows // heads // 2
    factor = LOG2E * width**-0.5
    starts = [jnp.int32(0)]
    for r in range(lengths_ref.shape[0] - 1):
        starts.append(starts[-1] + lengths_ref[r])

    def begin_of(position):
        begin = jnp.zeros_like(position)
        for start in starts[1:]:
            begin = jnp.where(start <= position, start, begin)
        return begin

    spans = []
    part_keys = pieces[0][0].shape[1] // 2
    in_part = lax.broadcasted_iota(jnp.int32, (1, part_keys), 1)
    in_part = in_part + jnp.where(in_part >= HALF_TOKENS, BLK - HALF_TOKENS, 0)
    local_of = {True: in_part + HALF_TOKENS * (1 - pair), False: in_part + HALF_TOKENS * pair}
    for number, ((shift, kinds), held) in enumerate(zip(sources, pieces)):
        lead = order_ref[lax.rem(shard + shift, span_total // 2)]
        parts = []
        for half, span in enumerate((lead, span_total - 1 - lead)):
            part = pl.ds(half * part_keys, part_keys)
            for piece, kind in zip(held, kinds):
                parts.append((piece, part, span * half_rows + local_of[kind]))
                row = (len(parts) - 1) * part_keys
                values_ref[number, pl.ds(row, part_keys), :] = piece[1, part, :]
        spans.append((lead, span_total - 1 - lead, parts))

    tile_tokens = Q_TILE // heads
    tiles_half = half_rows // tile_tokens

    def tile(index, _):
        at = pl.ds(pl.multiple_of(index * Q_TILE, Q_TILE), Q_TILE)
        own_lead = order_ref[shard]
        query_span = jnp.where(index < tiles_half, own_lead, span_total - 1 - own_lead)
        first_pos = query_span * half_rows + lax.rem(index, tiles_half) * tile_tokens
        begin_low = begin_of(first_pos)
        near = []
        for leading, trailing, parts in spans:
            lead_near, trail_near = (
                (span * half_rows <= first_pos + tile_tokens - 1)
                & (span * half_rows + half_rows - 1 >= begin_low)
                for span in (leading, trailing)
            )
            middle = len(parts) // 2
            near.append((lead_near & trail_near, 0, 2 * middle))
            near.append((lead_near & jnp.logical_not(trail_near), 0, middle))
            near.append((trail_near & jnp.logical_not(lead_near), middle, 2 * middle))
            near.append((jnp.logical_not(lead_near | trail_near), 0, 0))

        def state_of(number, strip, rows_at):
            if number > 0:
                return top_ref[strip, :], total_ref[strip, :], summed_ref[strip, :]
            if not first:
                return peak_in[rows_at, :], total_in[rows_at, :], summed_in[rows_at, :]
            empty = jnp.zeros((STRIP, width), jnp.float32)
            return empty + FLOOR, empty, empty

        def put_state(number, strip, rows_at, state):
            if number < len(spans) - 1:
                top_ref[strip, :], total_ref[strip, :], summed_ref[strip, :] = state
            elif last:
                whole = jnp.sum(state[1], axis=1, keepdims=True)
                result_ref[rows_at, :] = (state[2] / whole).astype(jnp.bfloat16)
            else:
                peak_out[rows_at, :], total_out[rows_at, :], summed_out[rows_at, :] = state

        for branch, (seen, start, end) in enumerate(near):
            number = branch // 4
            parts = spans[number][2][start:end]
            values_at = pl.ds(start * part_keys, (end - start) * part_keys)

            @pl.when(seen)
            def _():
                if not parts:
                    if 0 < number < len(spans) - 1:
                        return
                    for row in range(0, Q_TILE, STRIP):
                        strip = pl.ds(row, STRIP)
                        rows_at = pl.ds(pl.multiple_of(index * Q_TILE + row, STRIP), STRIP)
                        put_state(number, strip, rows_at, state_of(number, strip, rows_at))
                    return
                keys = jnp.concatenate([piece[0, part, :] for piece, part, _ in parts], axis=0)
                key_pos = [positions for _, _, positions in parts]
                index_in = lax.broadcasted_iota(jnp.int32, (STRIP, width), 0) // heads
                for row in range(0, Q_TILE, STRIP):
                    strip = pl.ds(row, STRIP)
                    rows_at = pl.ds(pl.multiple_of(index * Q_TILE + row, STRIP), STRIP)
                    score = lax.dot_general(
                        query_ref[rows_at, :],
                        keys,
                        (((1,), (1,)), ((), ())),
                        preferred_element_type=jnp.float32,
                    )
                    query_pos = first_pos + row // heads + index_in
                    query_begin = begin_of(query_pos)
                    old, total, summed = state_of(number, strip, rows_at)
                    top = old
                    masked = []
                    for which, at_key in enumerate(key_pos):
                        column = which * width
                        visible = (at_key <= query_pos) & (at_key >= query_begin)
                        masked.append(
                            jnp.where(visible, score[:, column : column + width], MASKED)
                        )
                        top = jnp.maximum(top, masked[-1])
                    peak = jnp.broadcast_to(
                        jnp.max(top, axis=1, keepdims=True), (STRIP, width)
                    )
                    fade = jnp.exp2((old - peak) * factor)
                    total = total * fade
                    weights = []
                    for part_score in masked:
                        weight = jnp.exp2((part_score - peak) * factor)
                        total = total + weight
                        weights.append(weight.astype(jnp.bfloat16))
                    summed = summed * fade + jnp.dot(
                        jnp.concatenate(weights, axis=1),
                        values_ref[number, values_at, :],
                        preferred_element_type=jnp.float32,
                    )
                    put_state(number, strip, rows_at, (peak, total, summed))

        if last:
            for number in range(Q_TILE // STRIP):
                send_strip(index * (Q_TILE // STRIP) + number).start()
        return 0

    lax.fori_loop(0, rows // Q_TILE, tile, 0)
    if last:
        for number in range(rows // STRIP):
            send_strip(number).wait()


def attend(order, lengths, partner, query, pieces, sources, state, last, heads):
    rows, width = query.shape
    first = state is None
    smem = pl.BlockSpec(memory_space=pltpu.SMEM)
    vmem = pl.BlockSpec(memory_space=pltpu.VMEM)
    state = () if first else state
    if last:
        out_shape = jax.ShapeDtypeStruct((rows, width), jnp.bfloat16)
        out_specs = pl.BlockSpec(memory_space=pltpu.HBM)
        sending = [
            pltpu.VMEM((rows, width), jnp.bfloat16),
            pltpu.SemaphoreType.DMA((rows // STRIP,)),
        ]
    else:
        sending = []
        out_shape = (jax.ShapeDtypeStruct((rows, width), jnp.float32),) * 3
        out_specs = (vmem,) * 3
    keys_each = pieces[0].shape[-2]
    count = len(sources)
    tile = pltpu.VMEM((Q_TILE, width), jnp.float32)
    return pl.pallas_call(
        functools.partial(attend_kernel, sources, first, last, 2 * order.shape[0], heads),
        out_shape=out_shape,
        in_specs=[smem] * 3 + [vmem] * (1 + len(pieces) + len(state)),
        out_specs=out_specs,
        scratch_shapes=[
            pltpu.VMEM((count, 2 * keys_each, width), jnp.bfloat16),
            tile,
            tile,
            tile,
        ]
        + sending,
        cost_estimate=pl.CostEstimate(
            flops=COST_FLOPS, bytes_accessed=4 * rows * width, transcendentals=0
        ),
        compiler_params=pltpu.CompilerParams(vmem_limit_bytes=24 * 2**20),
        name="attend",
    )(order, lengths, partner, query, *pieces, *state)


def locate_slots(order_ref, partner_ref, found, shard, shard_count):
    for slot in range(CAP):
        found[0, slot] = -1
    for index in range(shard_count):
        lead = order_ref[index]
        shift = lax.rem(index - shard + shard_count, shard_count)
        found[1, lead] = shift
        found[2, lead] = 0
        found[1, 2 * shard_count - 1 - lead] = shift
        found[2, 2 * shard_count - 1 - lead] = 1
    taken = jnp.int32(0)
    for block in range(partner_ref.shape[0]):
        mine = partner_ref[block] == shard

        @pl.when(mine)
        def _():
            found[0, taken] = block

        taken = taken + mine.astype(jnp.int32)


def slot_place(found, slot):
    block = found[0, slot]
    span = jnp.maximum(block, 0) // 2
    place = found[2, span] * 2 + lax.rem(jnp.maximum(block, 0), 2)
    return block >= 0, found[1, span], place * HALF_TOKENS


def gather_pieces(pieces, count, held):
    for index, piece in enumerate(pieces):
        held[index // count, index % count] = piece[...]


def pick_kernel(order_ref, partner_ref, *refs):
    given_ref, kept_ref, held, found = refs[-4:]
    count = held.shape[1]
    core = lax.axis_index("tp")
    share = HALF_TOKENS // 2
    gather_pieces(refs[: 2 * count], count, held)
    locate_slots(order_ref, partner_ref, found, lax.axis_index("ctx"), count)
    for slot in range(CAP):
        live, index, start = slot_place(found, slot)
        for out_ref, half in ((given_ref, 1 - core), (kept_ref, core)):
            begin = pl.ds(pl.multiple_of(start + half * share, share), share)
            for which in range(2):
                for kind in range(2):
                    rows = held[which, index, kind, begin, :]
                    out_ref[slot, kind, which] = jnp.where(live, rows, jnp.zeros_like(rows))


def pick(order, partner, stay, cross):
    smem = pl.BlockSpec(memory_space=pltpu.SMEM)
    vmem = pl.BlockSpec(memory_space=pltpu.VMEM)
    count = len(stay)
    piece_shape = cross[0].shape
    rows = jax.ShapeDtypeStruct((CAP, 2, 2, HALF_TOKENS // 2, piece_shape[2]), jnp.bfloat16)
    return pl.pallas_call(
        pick_kernel,
        out_shape=(rows, rows),
        in_specs=[smem, smem] + [vmem] * (2 * count),
        out_specs=(vmem, vmem),
        scratch_shapes=[
            pltpu.VMEM((2, count) + piece_shape, jnp.bfloat16),
            pltpu.SMEM((3, max(CAP, 2 * count)), jnp.int32),
        ],
        compiler_params=pltpu.CompilerParams(vmem_limit_bytes=12 * 2**20),
        name="pick_slots",
    )(order, partner, *stay, *cross)


def place_kernel(kept_ref, given_ref, out_ref, wide, result, sems):
    pair = lax.axis_index("pair")
    core = lax.axis_index("tp")
    share = kept_ref.shape[3]
    group_rows = wide.shape[0] // PLACE_GROUPS
    slots = CAP // PLACE_GROUPS
    copies = []
    for number in range(PLACE_GROUPS):
        for slot in range(number * slots, (number + 1) * slots):
            for kind in range(2):
                for which in range(2):
                    base = (slot * 2 + kind) * share * 4 + 2 * (pair if which == 0 else 1 - pair)
                    for ref, head in ((kept_ref, core), (given_ref, 1 - core)):
                        rows = ref[slot, kind, which].astype(jnp.float32)
                        wide[pl.ds(base + head, share, stride=4), :] = rows
        at = pl.ds(number * group_rows, group_rows)
        result[at, :] = wide[at, :].astype(jnp.bfloat16)
        copies.append(pltpu.make_async_copy(result.at[at, :], out_ref.at[at, :], sems.at[number]))
        copies[-1].start()
    for copy in copies:
        copy.wait()


def place(kept, given):
    rows, width = CAP * 2 * kept.shape[3] * 4, kept.shape[4]
    return pl.pallas_call(
        place_kernel,
        out_shape=jax.ShapeDtypeStruct((rows, width), jnp.bfloat16),
        out_specs=pl.BlockSpec(memory_space=pltpu.HBM),
        scratch_shapes=[
            pltpu.VMEM((rows, width), jnp.float32),
            pltpu.VMEM((rows, width), jnp.bfloat16),
            pltpu.SemaphoreType.DMA((PLACE_GROUPS,)),
        ],
        compiler_params=pltpu.CompilerParams(vmem_limit_bytes=12 * 2**20),
        name="place_slots",
    )(kept, given)


def ring(array, step, count):
    return lax.ppermute(array, "ctx", [(i, (i + step) % count) for i in range(count)])


def swap(array, axis):
    return lax.ppermute(array, axis, [(0, 1), (1, 0)])


def after(value, earlier):
    return lax.optimization_barrier((value, earlier))


def pieces_program(queries, keys, values, span_order, lengths, kv_partner):
    count = lax.axis_size("ctx")
    query_rows, heads, width = queries.shape
    partner = kv_partner[:, 0]
    query = queries.reshape(query_rows * heads, width)
    keys_flat = keys.reshape(-1, width)
    values_flat = values.reshape(-1, width)
    keys_other = swap(keys, "tp").reshape(-1, width)
    values_other = swap(values, "tp").reshape(-1, width)
    own = jnp.stack([keys_flat, values_flat]).astype(jnp.float32)
    cross0 = split_heads(own, keys_other, values_other, True)
    keys_other, _ = after(keys_other, cross0)
    stay0 = split_heads(own, keys_other, values_other, False)

    def step(pieces, sources, state, last=False):
        return attend(span_order, lengths, partner, query, pieces, sources, state, last, heads)

    both = (True, False)
    cross3 = ring(cross0, 1, count)
    cross1 = ring(cross0, -1, count)
    stay3 = ring(stay0, 1, count)
    stay1 = ring(stay0, -1, count)
    over0 = swap(cross0, "pair")
    state = step((cross0, stay0), ((0, both),), None)
    cross2 = ring(cross3, 1, count)
    over3 = swap(cross3, "pair")
    over1 = swap(cross1, "pair")
    stay2 = ring(stay3, 1, count)
    state = step((cross3, stay3, cross1, stay1), ((3, both), (1, both)), state)
    over2 = swap(cross2, "pair")
    stay = (stay0, stay1, stay2, stay3)
    over = (over0, over1, over2, over3)
    picked, kept = pick(span_order, partner, stay, over)
    given = swap(picked, "tp")
    cross2, _ = after(cross2, picked)
    attended = step((cross2, stay2), ((2, both),), state, True)
    cache = place(kept, given)
    return attended.reshape(queries.shape), cache.reshape(CAP, 2, HALF_TOKENS // 2, 4, width)


def pick_program(mesh):
    sizes = mesh.shape
    fits = sizes["ctx"] == 4 and sizes["pair"] == 2 and sizes["tp"] == 2
    return pieces_program if fits else shards


def solution(mesh):
    return jax.shard_map(
        pick_program(mesh),
        mesh=mesh,
        in_specs=(
            P(("groups", "ctx"), ("pair", "tp"), None),
            P(("groups", "ctx", "tp"), "pair", None),
            P(("groups", "ctx", "tp"), "pair", None),
            P("groups"),
            P("groups"),
            P("groups", None),
        ),
        out_specs=(
            P(("groups", "ctx"), ("pair", "tp"), None),
            P(("groups", "ctx"), None, ("pair", "tp"), None, None),
        ),
        check_vma=False,
    )
```
